32 devices in a mesh: ctx: 16 (over z, y, x), dp: 2 (over core).
Axes of the slice: x: 2, y: 2, z: 4, core: 2. Of those that a mesh axis runs over, the one named last changes fastest.
Arguments:
- queries: bfloat16 [2, 2048, 4096], P('dp', 'ctx'), may hold values from -9 to 9
- keys: bfloat16 [2, 2048, 512], P('dp', 'ctx'), may hold values from -6 to 6
- values: bfloat16 [2, 2048, 512], P('dp', 'ctx'), may hold values from -6 to 6
- output_gradient: bfloat16 [2, 2048, 4096], P('dp', 'ctx'), may hold values from -6 to 6
- adapter_query_down: bfloat16 [2, 2048, 16], P('dp', 'ctx'), may hold values from -0.29882812 to 0.29882812
- adapter_value_down: bfloat16 [2, 2048, 16], P('dp', 'ctx'), may hold values from -0.029907227 to 0.029907227
Outputs:
- query_gradient: bfloat16 [2, 2048, 4096], P('dp', 'ctx')
- key_gradient: bfloat16 [2, 2048, 512], P('dp', 'ctx')
- value_gradient: bfloat16 [2, 2048, 512], P('dp', 'ctx')
- adapter_query_up_gradient: float32 [16, 4096], replicated
- adapter_value_up_gradient: float32 [16, 512], replicated
The draws below stay inside these ranges and needn't reach their ends.
All inputs are finite; a program needn't handle non-finite values.
Results may differ from the reference program's by a relative error of at most 0.009.
Values may be sent and summed in bfloat16 or wider, within the bound.
A program may use at most 64 MiB of HBM per device.

```python
import jax
import jax.numpy as jnp
from jax import lax

QUERY_HEAD_COUNT = 32
KEY_VALUE_HEADS = 4
HEAD_WIDTH = 128
ADAPTER_RANK = 16
TOK_DEV = 128
GROUP = 512
TOKEN_LENGTH = 2048
BATCH_COUNT = 2


def draw_queries(key, part):
    key = jax.random.fold_in(key, 11)
    shape = (BATCH_COUNT, TOKEN_LENGTH, QUERY_HEAD_COUNT, HEAD_WIDTH)
    field = jnp.clip(jax.random.normal(key, shape, jnp.float32), -6.0, 6.0)
    return field.reshape(BATCH_COUNT, TOKEN_LENGTH, QUERY_HEAD_COUNT * HEAD_WIDTH).astype(jnp.bfloat16)


def draw_keys(key, part):
    key = jax.random.fold_in(key, 23)
    shape = (BATCH_COUNT, TOKEN_LENGTH, KEY_VALUE_HEADS, HEAD_WIDTH)
    field = jnp.clip(jax.random.normal(key, shape, jnp.float32), -6.0, 6.0)
    return field.reshape(BATCH_COUNT, TOKEN_LENGTH, KEY_VALUE_HEADS * HEAD_WIDTH).astype(jnp.bfloat16)


def levels(own_key, shape, shards, least, high):
    gain, own = 1.0, jax.random.fold_in(own_key, 6)
    for dim, shards_of in shards:
        steps = jnp.exp(jax.random.uniform(jax.random.fold_in(own, dim), (shards_of,), jnp.float32, least / len(shards), high / len(shards)))
        gain = gain * jnp.repeat(steps, shape[dim] // shards_of).reshape([-1 if axis == dim else 1 for axis in range(len(shape))])
    return gain


def normal_values(stream_key, shape, scale, bound, shards=(), kind=jnp.bfloat16):
    result = jax.random.normal(stream_key, shape, jnp.float32) * scale
    if len(shards) > 0:
        result = levels(stream_key, shape, shards, -0.22, 0.18) * result
    return jnp.clip(result, min=-bound, max=bound).astype(kind)


def setup_inputs(seed: int = 0) -> dict:
    streams_of = jax.random.split(jax.random.key(seed), 7)
    return {
        "queries": draw_queries(jax.random.fold_in(streams_of[6], 71), 0),
        "keys": draw_keys(jax.random.fold_in(streams_of[6], 71), 0),
        "values": normal_values(streams_of[2], (BATCH_COUNT, TOKEN_LENGTH, KEY_VALUE_HEADS * HEAD_WIDTH), 1.0, 6.0, ((0, 2), (1, 16))),
        "output_gradient": normal_values(streams_of[3], (BATCH_COUNT, TOKEN_LENGTH, QUERY_HEAD_COUNT * HEAD_WIDTH), 1.0, 6.0, ((0, 2), (1, 16))),
        "adapter_query_down": normal_values(streams_of[4], (BATCH_COUNT, TOKEN_LENGTH, ADAPTER_RANK), 0.05, 0.29882812, ((0, 2), (1, 16))),
        "adapter_value_down": normal_values(streams_of[5], (BATCH_COUNT, TOKEN_LENGTH, ADAPTER_RANK), 0.005, 0.029907227, ((0, 2), (1, 16))),
    }


ADAPTER_SCALE = 2.0


def group_grads(block):
    queries, keys, values, output_gradient = block
    size = queries.shape[0]
    kv_count = keys.shape[1]
    per_head = queries.shape[1] // kv_count
    blocks = size // TOK_DEV
    highest_precision = lax.Precision.HIGHEST
    query_wide = queries.astype(jnp.float32).reshape(size, kv_count, per_head, HEAD_WIDTH).transpose(1, 2, 0, 3)
    output_gradient_wide = output_gradient.astype(jnp.float32).reshape(size, kv_count, per_head, HEAD_WIDTH).transpose(1, 2, 0, 3)
    key_wide = keys.astype(jnp.float32).transpose(1, 0, 2)
    value_wide = values.astype(jnp.float32).transpose(1, 0, 2)
    softmax_scale = HEAD_WIDTH ** -0.5
    score_matrix = jnp.einsum("bvxj,bej->bvxe", query_wide, key_wide, precision=highest_precision) * softmax_scale
    causal = jnp.arange(size)[:, None] >= jnp.arange(size)[None, :]
    score_matrix = jnp.where(causal[None, None], score_matrix, -1e30)
    top = jnp.max(score_matrix, axis=-1, keepdims=True)
    raised = jnp.exp(score_matrix - top)
    probs = raised / jnp.sum(raised, axis=-1, keepdims=True)
    attention_weights = lax.optimization_barrier(probs.astype(jnp.bfloat16)).astype(jnp.float32)
    attended_output = jnp.einsum("ojcu,oue->ojce", attention_weights, value_wide, precision=highest_precision)
    delta = jnp.sum(output_gradient_wide * attended_output, axis=-1, keepdims=True)
    score_gradient = jnp.einsum("bvxj,bej->bvxe", output_gradient_wide, value_wide, precision=highest_precision)
    logit_gradient = lax.optimization_barrier((probs * (score_gradient - delta)).astype(jnp.bfloat16)).astype(jnp.float32)
    query_gradient = jnp.einsum("ojcu,oue->ojce", logit_gradient, key_wide, precision=highest_precision) * softmax_scale
    shape_b = (kv_count, per_head, blocks, TOK_DEV)
    logit_b = logit_gradient.reshape(shape_b + (size,))
    weights_b = attention_weights.reshape(shape_b + (size,))
    query_b = query_wide.reshape(shape_b + (HEAD_WIDTH,))
    grad_b = output_gradient_wide.reshape(shape_b + (HEAD_WIDTH,))
    key_blocks = jnp.einsum("grbus,grbud->bgsd", logit_b, query_b, precision=highest_precision) * softmax_scale
    value_blocks = jnp.einsum("grbus,grbud->bgsd", weights_b, grad_b, precision=highest_precision)
    key_blocks = lax.optimization_barrier(key_blocks.astype(jnp.bfloat16)).astype(jnp.float32)
    value_blocks = lax.optimization_barrier(value_blocks.astype(jnp.bfloat16)).astype(jnp.float32)
    key_gradient = jnp.sum(key_blocks, axis=0)
    value_gradient = jnp.sum(value_blocks, axis=0)
    query_gradient = query_gradient.transpose(2, 0, 1, 3).reshape(size, kv_count * per_head, HEAD_WIDTH).astype(jnp.bfloat16)
    key_gradient = key_gradient.transpose(1, 0, 2).astype(jnp.bfloat16)
    value_gradient = value_gradient.transpose(1, 0, 2).astype(jnp.bfloat16)
    return query_gradient, key_gradient, value_gradient


def to_groups(array):
    return array.reshape(TOKEN_LENGTH // GROUP, GROUP, array.shape[1], array.shape[2])


def from_groups(array):
    return array.reshape(TOKEN_LENGTH, array.shape[2], array.shape[3])


def half_grads(queries, keys, values, output_gradient):
    grads = lax.map(group_grads, (to_groups(queries), to_groups(keys), to_groups(values), to_groups(output_gradient)))
    return tuple(from_groups(piece) for piece in grads)


def sequence_grads(block):
    queries, keys, values, output_gradient = block
    queries = queries.reshape(TOKEN_LENGTH, QUERY_HEAD_COUNT, HEAD_WIDTH)
    output_gradient = output_gradient.reshape(TOKEN_LENGTH, QUERY_HEAD_COUNT, HEAD_WIDTH)
    keys = keys.reshape(TOKEN_LENGTH, KEY_VALUE_HEADS, HEAD_WIDTH)
    values = values.reshape(TOKEN_LENGTH, KEY_VALUE_HEADS, HEAD_WIDTH)
    query_half = QUERY_HEAD_COUNT // 2
    key_half = KEY_VALUE_HEADS // 2
    plain = half_grads(queries[:, :query_half], keys[:, :key_half], values[:, :key_half], output_gradient[:, :query_half])
    offset = GROUP // 2
    rolled = half_grads(jnp.roll(queries[:, query_half:], -offset, 0), jnp.roll(keys[:, key_half:], -offset, 0),
                        jnp.roll(values[:, key_half:], -offset, 0), jnp.roll(output_gradient[:, query_half:], -offset, 0))
    rolled = tuple(jnp.roll(piece, offset, 0) for piece in rolled)
    query_gradient = jnp.concatenate([plain[0], rolled[0]], axis=1).reshape(TOKEN_LENGTH, QUERY_HEAD_COUNT * HEAD_WIDTH)
    key_gradient = jnp.concatenate([plain[1], rolled[1]], axis=1).reshape(TOKEN_LENGTH, KEY_VALUE_HEADS * HEAD_WIDTH)
    value_gradient = jnp.concatenate([plain[2], rolled[2]], axis=1).reshape(TOKEN_LENGTH, KEY_VALUE_HEADS * HEAD_WIDTH)
    return query_gradient, key_gradient, value_gradient


def reference(queries, keys, values, output_gradient, adapter_query_down, adapter_value_down):
    query_gradient, key_gradient, value_gradient = lax.map(sequence_grads, (queries, keys, values, output_gradient))
    adapter_query_up_gradient = ADAPTER_SCALE * jnp.dot(adapter_query_down.reshape(-1, ADAPTER_RANK).T, query_gradient.reshape(-1, QUERY_HEAD_COUNT * HEAD_WIDTH),
                                           preferred_element_type=jnp.float32)
    adapter_value_up_gradient = ADAPTER_SCALE * jnp.dot(adapter_value_down.reshape(-1, ADAPTER_RANK).T, value_gradient.reshape(-1, KEY_VALUE_HEADS * HEAD_WIDTH),
                                           preferred_element_type=jnp.float32)
    return query_gradient, key_gradient, value_gradient, adapter_query_up_gradient, adapter_value_up_gradient
```

```python
import functools

import jax
import jax.numpy as jnp
from jax import lax
from jax.experimental import pallas as pl
from jax.experimental.pallas import tpu as pltpu
from jax.sharding import PartitionSpec as P

KEY_VALUE_HEADS = 4
PER_HEAD = 8
WIDTH = 128
ROWS = 128
RANK = 16
PLACES = 4
HALF_KEYS = 256
HALF_QUERIES = 2048
PLANE = 8
TILES = 5
VALUE_TILE = 2
ADAPTER_SCALE = 2.0
SCALE = WIDTH ** (-0.5)
LOG2E = 1.4426950408889634
MESH = pl.DeviceIdType.MESH
NT = (((1,), (1,)), ((), ()))
TN = (((0,), (0,)), ((), ()))
NN = (((1,), (0,)), ((), ()))


def matmul(a, b, dims):
    return lax.dot_general(a, b, dims, preferred_element_type=jnp.float32)


def kernel(
    ctx_size, dp_size,
    q_hbm, k_hbm, v_hbm, g_hbm, aq_hbm, av_hbm,
    dq_hbm, dk_out, dv_out, uq_out, uv_out,
    q_buf, g_buf, aq_buf, dq_buf, k_buf, v_buf, av_buf, w_buf, l_buf,
    part, arrived, l1_send, l1_recv, l2_recv, l3_recv,
    load_sem, own_sem, dq_sem, kv_send, kv_recv, ret_send, ret_recv,
    l1_ssem, l1_rsem, l2_ssem, l2_rsem, l3_ssem, l3_rsem,
):
    i = lax.axis_index("ctx")
    d = lax.axis_index("dp")
    g = i % PLACES
    group = i // PLACES
    parity = g % 2
    first = g // 2
    pairs = dp_size // 2
    me = g * 2 + d % 2
    planes = (ctx_size // PLACES) * pairs
    my_plane = group * pairs + d // 2

    def place_of(h):
        return (g + 2 * h) % PLACES

    def ahead(distance):
        return ((i + distance + ctx_size) % ctx_size, d)

    def plane_peer(e):
        return (group * PLACES + e // 2, (d // 2) * 2 + e % 2)

    def other_plane(r):
        return ((r // pairs) * PLACES + g, (r % pairs) * 2 + d % 2)

    def own_copies(h):
        p = place_of(h)
        cols = pl.ds(h * HALF_KEYS, HALF_KEYS)
        return [
            pltpu.make_async_copy(k_hbm.at[:, cols], k_buf.at[h, p], own_sem.at[h, 0]),
            pltpu.make_async_copy(v_hbm.at[:, cols], v_buf.at[h, p], own_sem.at[h, 1]),
            pltpu.make_async_copy(av_hbm, av_buf.at[h, p], own_sem.at[h, 2]),
        ]

    def query_copies(h):
        cols = pl.ds(pl.multiple_of(h * HALF_QUERIES, HALF_QUERIES), HALF_QUERIES)
        return [
            pltpu.make_async_copy(q_hbm.at[:, cols], q_buf.at[:, cols], load_sem.at[h, 0]),
            pltpu.make_async_copy(g_hbm.at[:, cols], g_buf.at[:, cols], load_sem.at[h, 1]),
        ]

    rank_copy = pltpu.make_async_copy(aq_hbm, aq_buf, load_sem.at[0, 2])
    for h in range(2):
        for copy in own_copies(h):
            copy.start()
    for copy in query_copies(first):
        copy.start()
    rank_copy.start()
    for copy in query_copies(1 - first):
        copy.start()

    barrier = pltpu.get_barrier_semaphore()

    def greet(device):
        pl.semaphore_signal(barrier, inc=1, device_id=device, device_id_type=MESH)

    for r in range(1, PLANE):
        greet(plane_peer((me + r) % PLANE))
    for r in range(1, planes):
        greet(other_plane((my_plane + r) % planes))
    beside = (group * PLACES + jnp.where(first == 0, -2, PLACES) + ctx_size) % ctx_size
    greet((beside, d))
    greet((beside + 1, d))
    pl.semaphore_wait(barrier, PLANE - 1 + planes - 1 + 2)

    def key_copies(h, p, distance):
        cols = pl.ds(h * HALF_KEYS, HALF_KEYS)
        target = ahead(distance)
        pieces = (
            (k_hbm.at[:, cols], k_buf.at[h, p]),
            (v_hbm.at[:, cols], v_buf.at[h, p]),
            (av_hbm, av_buf.at[h, p]),
        )
        return [
            pltpu.make_async_remote_copy(
                src_ref=src,
                dst_ref=dst,
                send_sem=kv_send.at[h, distance - 1, n],
                recv_sem=kv_recv.at[h, p, n],
                device_id=target,
                device_id_type=MESH,
            )
            for n, (src, dst) in enumerate(pieces)
        ]

    def key_arrivals(h, b):
        pieces = (k_buf.at[h, b], v_buf.at[h, b], av_buf.at[h, b])
        return [
            pltpu.make_async_remote_copy(
                src_ref=dst,
                dst_ref=dst,
                send_sem=kv_send.at[h, 0, n],
                recv_sem=kv_recv.at[h, b, n],
                device_id=ahead(1),
                device_id_type=MESH,
            )
            for n, dst in enumerate(pieces)
        ]

    for distance in range(1, PLACES):
        for h in range(2):
            p = place_of(h)

            @pl.when(p + distance < PLACES)
            def _():
                for copy in key_copies(h, p, distance):
                    copy.start()

    def return_copy(h, c, b, blocks):
        return pltpu.make_async_remote_copy(
            src_ref=part.at[h, c, b],
            dst_ref=arrived.at[h, c, blocks - 2],
            send_sem=ret_send.at[h, c, b],
            recv_sem=ret_recv.at[h, c, blocks - 2],
            device_id=ahead(b - (blocks - 1)),
            device_id_type=MESH,
        )

    def return_arrival(h, c, slot):
        return pltpu.make_async_remote_copy(
            src_ref=arrived.at[h, c, slot],
            dst_ref=arrived.at[h, c, slot],
            send_sem=ret_send.at[h, c, 0],
            recv_sem=ret_recv.at[h, c, slot],
            device_id=ahead(1),
            device_id_type=MESH,
        )

    def dq_copy(h, c):
        cols = pl.ds(pl.multiple_of((2 * h + c) * PER_HEAD * WIDTH, PER_HEAD * WIDTH), PER_HEAD * WIDTH)
        return pltpu.make_async_copy(dq_buf.at[:, cols], dq_hbm.at[:, cols], dq_sem.at[h, c])

    def head_step(h, c, blocks):
        span = blocks * ROWS
        cols = pl.ds(pl.multiple_of(c * WIDTH, WIDTH), WIDTH)
        base = (2 * h + c) * PER_HEAD * WIDTH

        def head_cols(t):
            return pl.ds(pl.multiple_of(base + t * WIDTH, WIDTH), WIDTH)

        keys = k_buf[h, :blocks, :, cols].reshape(span, WIDTH)
        vals = v_buf[h, :blocks, :, cols].reshape(span, WIDTH)
        key_row = lax.broadcasted_iota(jnp.int32, (ROWS, 2 * ROWS), 0)
        query_col = lax.broadcasted_iota(jnp.int32, (ROWS, 2 * ROWS), 1) % ROWS
        allowed = key_row <= query_col

        def pair(buf, t):
            return jnp.concatenate([buf[:, head_cols(2 * t)], buf[:, head_cols(2 * t + 1)]], axis=0)

        for t in range(PER_HEAD // 2):
            q = pair(q_buf, t)
            grad = pair(g_buf, t)
            s = matmul(keys, q, NT)
            last = jnp.where(allowed, s[span - ROWS:], -1e30)
            s = last if blocks == 1 else jnp.concatenate([s[: span - ROWS], last], axis=0)
            top = jnp.max(s, axis=0, keepdims=True)
            raised = jnp.exp2((s - top) * (SCALE * LOG2E))
            probs = raised * (1.0 / jnp.sum(raised, axis=0, keepdims=True))
            weights = probs.astype(jnp.bfloat16)
            score_grad = matmul(vals, grad, NT)
            delta = jnp.sum(weights.astype(jnp.float32) * score_grad, axis=0, keepdims=True)
            logit = (probs * (score_grad - delta)).astype(jnp.bfloat16)
            w_buf[:span, 2 * t * ROWS:(2 * t + 2) * ROWS] = weights
            l_buf[:span, 2 * t * ROWS:(2 * t + 2) * ROWS] = logit
        q_all = jnp.concatenate([q_buf[:, head_cols(t)] for t in range(PER_HEAD)], axis=0)
        grad_all = jnp.concatenate([g_buf[:, head_cols(t)] for t in range(PER_HEAD)], axis=0)
        logit_all = l_buf[:span, :]
        dk = (matmul(logit_all, q_all, NN) * SCALE).astype(jnp.bfloat16)
        dv = matmul(w_buf[:span, :], grad_all, NN).astype(jnp.bfloat16)
        for b in range(blocks):
            part[h, c, b, 0] = dk[b * ROWS:(b + 1) * ROWS]
            part[h, c, b, 1] = dv[b * ROWS:(b + 1) * ROWS]
        for b in range(blocks - 1):
            return_copy(h, c, b, blocks).start()
        dq = (matmul(logit_all, keys, TN) * SCALE).astype(jnp.bfloat16)
        for t in range(PER_HEAD):
            dq_buf[:, head_cols(t)] = dq[t * ROWS:(t + 1) * ROWS]
        dq_copy(h, c).start()
        down = aq_buf[...]
        for t in range(PER_HEAD):
            l1_send[t, 3 * h + c] = matmul(down, dq[t * ROWS:(t + 1) * ROWS], TN).astype(jnp.bfloat16)
        value_down = av_buf[h, :blocks].reshape(span, RANK)
        up = matmul(value_down, dv, TN).astype(jnp.bfloat16)
        kv = 2 * h + c
        l1_send[2 * kv, VALUE_TILE] = up
        l1_send[2 * kv + 1, VALUE_TILE] = up

    def stage(h, blocks):
        for b in range(blocks - 1):
            for copy in key_arrivals(h, b):
                copy.wait_recv()

        def one(c, carry):
            head_step(h, c, blocks)
            return carry

        lax.fori_loop(0, 2, one, 0)

    def l1_copy(n, e_from, h_from, r, target):
        start, count = (3 * h_from, 2) if n == 0 else (2 * h_from, 3)
        tiles = pl.ds(start, count)
        return pltpu.make_async_remote_copy(
            src_ref=l1_send.at[target, tiles],
            dst_ref=l1_recv.at[e_from, tiles],
            send_sem=l1_ssem.at[n, r - 1],
            recv_sem=l1_rsem.at[n, e_from],
            device_id=plane_peer(target),
            device_id_type=MESH,
        )

    def l1_start(n, h):
        for r in range(1, PLANE):
            l1_copy(n, me, h, r, (me + r) % PLANE).start()

    second = 1 - first
    for copy in own_copies(0) + own_copies(1):
        copy.wait()
    for copy in query_copies(first):
        copy.wait()
    rank_copy.wait()
    for blocks in (1, 2):
        pl.when(parity == blocks - 1)(functools.partial(stage, first, blocks))
    l1_start(0, first)
    for copy in query_copies(second):
        copy.wait()
    for blocks in (3, 4):
        pl.when(parity == blocks - 3)(functools.partial(stage, second, blocks))
    l1_start(1, second)

    total = l1_send[me].astype(jnp.float32)
    for r in range(1, PLANE):
        e = (me + r) % PLANE
        l1_copy(0, e, e // 4, r, me).wait_recv()
        l1_copy(1, e, 1 - e // 4, r, me).wait_recv()
        total = total + l1_recv[e].astype(jnp.float32)
    l2_recv[my_plane] = total.astype(jnp.bfloat16)

    def l2_copy(r, origin, target):
        return pltpu.make_async_remote_copy(
            src_ref=l2_recv.at[origin],
            dst_ref=l2_recv.at[origin],
            send_sem=l2_ssem.at[r - 1],
            recv_sem=l2_rsem.at[origin],
            device_id=other_plane(target),
            device_id_type=MESH,
        )

    for r in range(1, planes):
        l2_copy(r, my_plane, (my_plane + r) % planes).start()

    def finish(h, place):
        for c in range(2):
            for slot in range(place, PLACES - 1):
                return_arrival(h, c, slot).wait_recv()
            cols = pl.ds(pl.multiple_of((2 * h + c) * WIDTH, WIDTH), WIDTH)
            for n, out in enumerate((dk_out, dv_out)):
                acc = part[h, c, place, n].astype(jnp.float32)
                for slot in range(place, PLACES - 1):
                    acc = acc + arrived[h, c, slot, n].astype(jnp.float32)
                out[:, cols] = acc.astype(jnp.bfloat16)

    for place in (2, 3):
        pl.when(parity == place - 2)(functools.partial(finish, second, place))

    for r in range(1, planes):
        l2_copy(r, (my_plane + r) % planes, my_plane).wait_recv()
    total = l2_recv[0].astype(jnp.float32)
    for r in range(1, planes):
        total = total + l2_recv[r].astype(jnp.float32)
    l3_recv[me] = (total * ADAPTER_SCALE).astype(jnp.bfloat16)

    def l3_copy(r, origin, target):
        return pltpu.make_async_remote_copy(
            src_ref=l3_recv.at[origin],
            dst_ref=l3_recv.at[origin],
            send_sem=l3_ssem.at[r - 1],
            recv_sem=l3_rsem.at[origin],
            device_id=plane_peer(target),
            device_id_type=MESH,
        )

    for r in range(1, PLANE):
        l3_copy(r, me, (me + r) % PLANE).start()
    for place in (0, 1):
        pl.when(parity == place)(functools.partial(finish, first, place))
    for r in range(1, PLANE):
        l3_copy(r, (me + r) % PLANE, me).wait_recv()
    for e in range(PLANE):
        for kv in range(KEY_VALUE_HEADS):
            head = kv * PER_HEAD + e
            uq_out[:, head * WIDTH:(head + 1) * WIDTH] = l3_recv[e, kv + kv // 2].astype(jnp.float32)
    for kv in range(KEY_VALUE_HEADS):
        uv_out[:, kv * WIDTH:(kv + 1) * WIDTH] = l3_recv[2 * kv, VALUE_TILE].astype(jnp.float32)

    for h in range(2):
        p = place_of(h)
        for distance in range(1, PLACES):

            @pl.when(p + distance < PLACES)
            def _():
                for copy in key_copies(h, p, distance):
                    copy.wait_send()

        for c in range(2):
            dq_copy(h, c).wait()

    def returned(h, blocks):
        for c in range(2):
            for b in range(blocks - 1):
                return_copy(h, c, b, blocks).wait_send()

    pl.when(parity == 1)(functools.partial(returned, first, 2))
    for blocks in (3, 4):
        pl.when(parity == blocks - 3)(functools.partial(returned, second, blocks))
    for r in range(1, PLANE):
        l1_copy(0, me, first, r, (me + r) % PLANE).wait_send()
        l1_copy(1, me, second, r, (me + r) % PLANE).wait_send()
        l3_copy(r, me, (me + r) % PLANE).wait_send()
    for r in range(1, planes):
        l2_copy(r, my_plane, (my_plane + r) % planes).wait_send()


def body(ctx_size, dp_size, queries, keys, values, output_gradient, query_down, value_down):
    planes = (ctx_size // PLACES) * (dp_size // 2)
    bf16, f32 = jnp.bfloat16, jnp.float32
    dma = pltpu.SemaphoreType.DMA
    anywhere = pl.BlockSpec(memory_space=pl.ANY)
    vmem = pl.BlockSpec(memory_space=pltpu.VMEM)
    wide = PER_HEAD * WIDTH
    outs = pl.pallas_call(
        functools.partial(kernel, ctx_size, dp_size),
        out_shape=(
            jax.ShapeDtypeStruct(queries.shape[1:], bf16),
            jax.ShapeDtypeStruct(keys.shape[1:], bf16),
            jax.ShapeDtypeStruct(values.shape[1:], bf16),
            jax.ShapeDtypeStruct((RANK, queries.shape[2]), f32),
            jax.ShapeDtypeStruct((RANK, values.shape[2]), f32),
        ),
        in_specs=[anywhere] * 6,
        out_specs=(anywhere, vmem, vmem, vmem, vmem),
        scratch_shapes=[
            pltpu.VMEM((ROWS, KEY_VALUE_HEADS * wide), bf16),
            pltpu.VMEM((ROWS, KEY_VALUE_HEADS * wide), bf16),
            pltpu.VMEM((ROWS, RANK), bf16),
            pltpu.VMEM((ROWS, KEY_VALUE_HEADS * wide), bf16),
            pltpu.VMEM((2, PLACES, ROWS, HALF_KEYS), bf16),
            pltpu.VMEM((2, PLACES, ROWS, HALF_KEYS), bf16),
            pltpu.VMEM((2, PLACES, ROWS, RANK), bf16),
            pltpu.VMEM((PLACES * ROWS, wide), bf16),
            pltpu.VMEM((PLACES * ROWS, wide), bf16),
            pltpu.VMEM((2, 2, PLACES, 2, ROWS, WIDTH), bf16),
            pltpu.VMEM((2, 2, PLACES - 1, 2, ROWS, WIDTH), bf16),
            pltpu.VMEM((PLANE, TILES, RANK, WIDTH), bf16),
            pltpu.VMEM((PLANE, TILES, RANK, WIDTH), bf16),
            pltpu.VMEM((planes, TILES, RANK, WIDTH), bf16),
            pltpu.VMEM((PLANE, TILES, RANK, WIDTH), bf16),
            dma((2, 3)),
            dma((2, 3)),
            dma((2, 2)),
            dma((2, PLACES - 1, 3)),
            dma((2, PLACES, 3)),
            dma((2, 2, PLACES)),
            dma((2, 2, PLACES - 1)),
            dma((2, PLANE - 1)),
            dma((2, PLANE)),
            dma((max(planes - 1, 1),)),
            dma((planes,)),
            dma((PLANE - 1,)),
            dma((PLANE,)),
        ],
        compiler_params=pltpu.CompilerParams(
            collective_id=0, has_side_effects=True, vmem_limit_bytes=40 * 1024 * 1024
        ),
        cost_estimate=pl.CostEstimate(
            flops=2_500_000_000, bytes_accessed=4_000_000, transcendentals=1_600_000
        ),
    )(queries[0], keys[0], values[0], output_gradient[0], query_down[0], value_down[0])
    return (outs[0][None], outs[1][None], outs[2][None], outs[3], outs[4])


def solution(mesh):
    spec = P("dp", "ctx", None)
    return jax.shard_map(
        functools.partial(body, mesh.shape["ctx"], mesh.shape["dp"]),
        mesh=mesh,
        in_specs=(spec,) * 6,
        out_specs=(spec, spec, spec, P(), P()),
        check_vma=False,
    )
```

```python
import functools

import jax
import jax.numpy as jnp
from jax import lax
from jax.experimental import pallas as pl
from jax.experimental.pallas import tpu as pltpu
from jax.sharding import PartitionSpec as P

KEY_VALUE_HEADS = 4
PER_HEAD = 8
WIDTH = 128
ROWS = 128
RANK = 16
PLACES = 4
HALF_KEYS = 256
HALF_QUERIES = 2048
PLANE = 8
TILES = 5
KEY_ROWS = slice(0, ROWS)
VALUE_ROWS = slice(ROWS, 2 * ROWS)
DOWN_ROWS = slice(2 * ROWS, 2 * ROWS + RANK)
VALUE_TILE = 2
ADAPTER_SCALE = 2.0
SCALE = WIDTH ** (-0.5)
LOG2E = 1.4426950408889634
MESH = pl.DeviceIdType.MESH
NT = (((1,), (1,)), ((), ()))
NN = (((1,), (0,)), ((), ()))


def matmul(a, b, dims):
    return lax.dot_general(a, b, dims, preferred_element_type=jnp.float32)


def kernel(
    ctx_size, dp_size,
    q_hbm, k_hbm, v_hbm, g_hbm, aq_hbm, av_hbm,
    dq_out, dk_out, dv_out, uq_out, uv_out,
    q_buf, g_buf, aq_buf, kv_buf, w_buf, l_buf,
    part, arrived, l1_send, l1_recv, l2_recv, l3_recv,
    load_sem, own_sem, kv_send, kv_recv, ret_send, ret_recv,
    l1_ssem, l1_rsem, l2_ssem, l2_rsem, l3_ssem, l3_rsem,
):
    i = lax.axis_index("ctx")
    d = lax.axis_index("dp")
    g = i % PLACES
    group = i // PLACES
    parity = g % 2
    first = g // 2
    pairs = dp_size // 2
    me = g * 2 + d % 2
    planes = (ctx_size // PLACES) * pairs
    my_plane = group * pairs + d // 2

    def place_of(h):
        return (g + 2 * h) % PLACES

    def ahead(distance):
        return ((i + distance + ctx_size) % ctx_size, d)

    def plane_peer(e):
        return (group * PLACES + e // 2, (d // 2) * 2 + e % 2)

    def other_plane(r):
        return ((r // pairs) * PLACES + g, (r % pairs) * 2 + d % 2)

    def own_copies(h):
        p = place_of(h)
        cols = pl.ds(h * HALF_KEYS, HALF_KEYS)
        return [
            pltpu.make_async_copy(k_hbm.at[:, cols], kv_buf.at[h, p, KEY_ROWS], own_sem.at[h, 0]),
            pltpu.make_async_copy(v_hbm.at[:, cols], kv_buf.at[h, p, VALUE_ROWS], own_sem.at[h, 1]),
            pltpu.make_async_copy(av_hbm, kv_buf.at[h, p, DOWN_ROWS, pl.ds(0, ROWS)], own_sem.at[h, 2]),
        ]

    def query_copies(h):
        cols = pl.ds(pl.multiple_of(h * HALF_QUERIES, HALF_QUERIES), HALF_QUERIES)
        return [
            pltpu.make_async_copy(q_hbm.at[:, cols], q_buf.at[:, cols], load_sem.at[h, 0]),
            pltpu.make_async_copy(g_hbm.at[:, cols], g_buf.at[:, cols], load_sem.at[h, 1]),
        ]

    rank_copy = pltpu.make_async_copy(aq_hbm, aq_buf, load_sem.at[0, 2])
    for h in range(2):
        for copy in own_copies(h):
            copy.start()
    for copy in query_copies(first):
        copy.start()
    rank_copy.start()
    for copy in query_copies(1 - first):
        copy.start()

    barrier = pltpu.get_barrier_semaphore()

    def greet(device):
        pl.semaphore_signal(barrier, inc=1, device_id=device, device_id_type=MESH)

    for r in range(1, PLANE):
        greet(plane_peer((me + r) % PLANE))
    for r in range(1, planes):
        greet(other_plane((my_plane + r) % planes))
    beside = (group * PLACES + jnp.where(first == 0, -2, PLACES) + ctx_size) % ctx_size
    greet((beside, d))
    greet((beside + 1, d))
    pl.semaphore_wait(barrier, PLANE - 1 + planes - 1 + 2)

    def key_copy(h, p, distance):
        return pltpu.make_async_remote_copy(
            src_ref=kv_buf.at[h, p],
            dst_ref=kv_buf.at[h, p],
            send_sem=kv_send.at[h, distance - 1],
            recv_sem=kv_recv.at[h, p],
            device_id=ahead(distance),
            device_id_type=MESH,
        )

    def key_arrival(h, b):
        return pltpu.make_async_remote_copy(
            src_ref=kv_buf.at[h, b],
            dst_ref=kv_buf.at[h, b],
            send_sem=kv_send.at[h, 0],
            recv_sem=kv_recv.at[h, b],
            device_id=ahead(1),
            device_id_type=MESH,
        )

    for copy in own_copies(0) + own_copies(1):
        copy.wait()
    for distance in range(1, PLACES):
        for h in range(2):
            p = place_of(h)

            @pl.when(p + distance < PLACES)
            def _():
                key_copy(h, p, distance).start()

    def return_copy(h, c, b, blocks):
        return pltpu.make_async_remote_copy(
            src_ref=part.at[h, c, b],
            dst_ref=arrived.at[h, c, blocks - 2],
            send_sem=ret_send.at[h, c, b],
            recv_sem=ret_recv.at[h, c, blocks - 2],
            device_id=ahead(b - (blocks - 1)),
            device_id_type=MESH,
        )

    def return_arrival(h, c, slot):
        return pltpu.make_async_remote_copy(
            src_ref=arrived.at[h, c, slot],
            dst_ref=arrived.at[h, c, slot],
            send_sem=ret_send.at[h, c, 0],
            recv_sem=ret_recv.at[h, c, slot],
            device_id=ahead(1),
            device_id_type=MESH,
        )

    def head_step(h, c, blocks):
        span = blocks * ROWS
        cols = pl.ds(pl.multiple_of(c * WIDTH, WIDTH), WIDTH)
        base = (2 * h + c) * PER_HEAD * WIDTH

        def head_cols(t):
            return pl.ds(pl.multiple_of(base + t * WIDTH, WIDTH), WIDTH)

        keys = kv_buf[h, :blocks, KEY_ROWS, cols].reshape(span, WIDTH)
        vals = kv_buf[h, :blocks, VALUE_ROWS, cols].reshape(span, WIDTH)
        key_row = lax.broadcasted_iota(jnp.int32, (ROWS, 2 * ROWS), 0)
        query_col = lax.broadcasted_iota(jnp.int32, (ROWS, 2 * ROWS), 1) % ROWS
        allowed = key_row <= query_col

        def pair(buf, t):
            return jnp.concatenate([buf[:, head_cols(2 * t)], buf[:, head_cols(2 * t + 1)]], axis=0)

        for t in range(PER_HEAD // 2):
            q = pair(q_buf, t)
            grad = pair(g_buf, t)
            s = matmul(keys, q, NT)
            last = jnp.where(allowed, s[span - ROWS:], -1e30)
            s = last if blocks == 1 else jnp.concatenate([s[: span - ROWS], last], axis=0)
            top = jnp.max(s, axis=0, keepdims=True)
            score_grad = matmul(vals, grad, NT)
            raised = jnp.exp2((s - top) * (SCALE * LOG2E))
            inverse = 1.0 / jnp.sum(raised, axis=0, keepdims=True)
            delta = jnp.sum(raised * score_grad, axis=0, keepdims=True) * inverse
            probs = raised * inverse
            weights = probs.astype(jnp.bfloat16)
            logit = (probs * (score_grad - delta)).astype(jnp.bfloat16)
            w_buf[:span, 2 * t * ROWS:(2 * t + 2) * ROWS] = weights
            l_buf[:span, 2 * t * ROWS:(2 * t + 2) * ROWS] = logit
        q_all = jnp.concatenate([q_buf[:, head_cols(t)] for t in range(PER_HEAD)], axis=0)
        grad_all = jnp.concatenate([g_buf[:, head_cols(t)] for t in range(PER_HEAD)], axis=0)
        logit_all = l_buf[:span, :]
        dk = (matmul(logit_all, q_all, NN) * SCALE).astype(jnp.bfloat16)
        dv = matmul(w_buf[:span, :], grad_all, NN).astype(jnp.bfloat16)
        for b in range(blocks):
            part[h, c, b, 0] = dk[b * ROWS:(b + 1) * ROWS]
            part[h, c, b, 1] = dv[b * ROWS:(b + 1) * ROWS]
        for b in range(blocks - 1):
            return_copy(h, c, b, blocks).start()
        dq = (matmul(keys.T, logit_all, NN) * SCALE).astype(jnp.bfloat16)
        for t in range(PER_HEAD):
            dq_out[:, head_cols(t)] = dq[:, t * ROWS:(t + 1) * ROWS].T
        wide = pl.ds(pl.multiple_of(base, PER_HEAD * WIDTH), PER_HEAD * WIDTH)
        up = matmul(aq_buf[...], dq_out[:, wide], NN).astype(jnp.bfloat16)
        for t in range(PER_HEAD):
            l1_send[t, 3 * h + c] = up[:, t * WIDTH:(t + 1) * WIDTH]
        value_down = jnp.concatenate([kv_buf[h, b, DOWN_ROWS, :ROWS] for b in range(blocks)], axis=1)
        up = matmul(value_down, dv, NN).astype(jnp.bfloat16)
        kv = 2 * h + c
        l1_send[2 * kv, VALUE_TILE] = up
        l1_send[2 * kv + 1, VALUE_TILE] = up

    def stage(h, blocks):
        for b in range(blocks - 1):
            key_arrival(h, b).wait_recv()

        def one(c, carry):
            head_step(h, c, blocks)
            return carry

        lax.fori_loop(0, 2, one, 0)

    def l1_copy(r, origin, target):
        return pltpu.make_async_remote_copy(
            src_ref=l1_send.at[target],
            dst_ref=l1_recv.at[origin],
            send_sem=l1_ssem.at[r - 1],
            recv_sem=l1_rsem.at[origin],
            device_id=plane_peer(target),
            device_id_type=MESH,
        )

    second = 1 - first
    for copy in query_copies(first):
        copy.wait()
    rank_copy.wait()
    for blocks in (1, 2):
        pl.when(parity == blocks - 1)(functools.partial(stage, first, blocks))
    for copy in query_copies(second):
        copy.wait()
    for blocks in (3, 4):
        pl.when(parity == blocks - 3)(functools.partial(stage, second, blocks))
    for r in range(1, PLANE):
        l1_copy(r, me, (me + r) % PLANE).start()

    total = l1_send[me].astype(jnp.float32)
    for r in range(1, PLANE):
        e = (me + r) % PLANE
        l1_copy(r, e, me).wait_recv()
        total = total + l1_recv[e].astype(jnp.float32)
    l2_recv[my_plane] = total.astype(jnp.bfloat16)

    def l2_copy(r, origin, target):
        return pltpu.make_async_remote_copy(
            src_ref=l2_recv.at[origin],
            dst_ref=l2_recv.at[origin],
            send_sem=l2_ssem.at[r - 1],
            recv_sem=l2_rsem.at[origin],
            device_id=other_plane(target),
            device_id_type=MESH,
        )

    for r in range(1, planes):
        l2_copy(r, my_plane, (my_plane + r) % planes).start()

    def finish(h, place):
        for c in range(2):
            for slot in range(place, PLACES - 1):
                return_arrival(h, c, slot).wait_recv()
            cols = pl.ds(pl.multiple_of((2 * h + c) * WIDTH, WIDTH), WIDTH)
            for n, out in enumerate((dk_out, dv_out)):
                acc = part[h, c, place, n].astype(jnp.float32)
                for slot in range(place, PLACES - 1):
                    acc = acc + arrived[h, c, slot, n].astype(jnp.float32)
                out[:, cols] = acc.astype(jnp.bfloat16)

    for place in (2, 3):
        pl.when(parity == place - 2)(functools.partial(finish, second, place))

    for r in range(1, planes):
        l2_copy(r, (my_plane + r) % planes, my_plane).wait_recv()
    total = l2_recv[0].astype(jnp.float32)
    for r in range(1, planes):
        total = total + l2_recv[r].astype(jnp.float32)
    l3_recv[me] = (total * ADAPTER_SCALE).astype(jnp.bfloat16)

    def l3_copy(r, origin, target):
        return pltpu.make_async_remote_copy(
            src_ref=l3_recv.at[origin],
            dst_ref=l3_recv.at[origin],
            send_sem=l3_ssem.at[r - 1],
            recv_sem=l3_rsem.at[origin],
            device_id=plane_peer(target),
            device_id_type=MESH,
        )

    for r in range(1, PLANE):
        l3_copy(r, me, (me + r) % PLANE).start()
    for place in (0, 1):
        pl.when(parity == place)(functools.partial(finish, first, place))
    for r in range(1, PLANE):
        l3_copy(r, (me + r) % PLANE, me).wait_recv()
    for e in range(PLANE):
        for kv in range(KEY_VALUE_HEADS):
            head = kv * PER_HEAD + e
            uq_out[:, head * WIDTH:(head + 1) * WIDTH] = l3_recv[e, kv + kv // 2].astype(jnp.float32)
    for kv in range(KEY_VALUE_HEADS):
        uv_out[:, kv * WIDTH:(kv + 1) * WIDTH] = l3_recv[2 * kv, VALUE_TILE].astype(jnp.float32)

    for h in range(2):
        p = place_of(h)
        for distance in range(1, PLACES):

            @pl.when(p + distance < PLACES)
            def _():
                key_copy(h, p, distance).wait_send()

    def returned(h, blocks):
        for c in range(2):
            for b in range(blocks - 1):
                return_copy(h, c, b, blocks).wait_send()

    pl.when(parity == 1)(functools.partial(returned, first, 2))
    for blocks in (3, 4):
        pl.when(parity == blocks - 3)(functools.partial(returned, second, blocks))
    for r in range(1, PLANE):
        l1_copy(r, me, (me + r) % PLANE).wait_send()
        l3_copy(r, me, (me + r) % PLANE).wait_send()
    for r in range(1, planes):
        l2_copy(r, my_plane, (my_plane + r) % planes).wait_send()


def write_out(*refs):
    sources, targets, sems = refs[:5], refs[5:10], refs[10]
    copies = [
        pltpu.make_async_copy(source, target, sems.at[n])
        for n, (source, target) in enumerate(zip(sources, targets))
    ]
    for copy in copies:
        copy.start()
    for copy in copies:
        copy.wait()


def body(ctx_size, dp_size, queries, keys, values, output_gradient, query_down, value_down):
    planes = (ctx_size // PLACES) * (dp_size // 2)
    bf16, f32 = jnp.bfloat16, jnp.float32
    dma = pltpu.SemaphoreType.DMA
    hbm = pl.BlockSpec(memory_space=pltpu.HBM)
    vmem = pl.BlockSpec(memory_space=pltpu.VMEM)
    wide = PER_HEAD * WIDTH
    outs = pl.pallas_call(
        functools.partial(kernel, ctx_size, dp_size),
        out_shape=(
            jax.ShapeDtypeStruct(queries.shape[1:], bf16),
            jax.ShapeDtypeStruct(keys.shape[1:], bf16),
            jax.ShapeDtypeStruct(values.shape[1:], bf16),
            jax.ShapeDtypeStruct((RANK, queries.shape[2]), f32),
            jax.ShapeDtypeStruct((RANK, values.shape[2]), f32),
        ),
        in_specs=[hbm] * 6,
        out_specs=(vmem,) * 5,
        scratch_shapes=[
            pltpu.VMEM((ROWS, KEY_VALUE_HEADS * wide), bf16),
            pltpu.VMEM((ROWS, KEY_VALUE_HEADS * wide), bf16),
            pltpu.VMEM((RANK, ROWS), bf16),
            pltpu.VMEM((2, PLACES, 2 * ROWS + RANK, HALF_KEYS), bf16),
            pltpu.VMEM((PLACES * ROWS, wide), bf16),
            pltpu.VMEM((PLACES * ROWS, wide), bf16),
            pltpu.VMEM((2, 2, PLACES, 2, ROWS, WIDTH), bf16),
            pltpu.VMEM((2, 2, PLACES - 1, 2, ROWS, WIDTH), bf16),
            pltpu.VMEM((PLANE, TILES, RANK, WIDTH), bf16),
            pltpu.VMEM((PLANE, TILES, RANK, WIDTH), bf16),
            pltpu.VMEM((planes, TILES, RANK, WIDTH), bf16),
            pltpu.VMEM((PLANE, TILES, RANK, WIDTH), bf16),
            dma((2, 3)),
            dma((2, 3)),
            dma((2, PLACES - 1)),
            dma((2, PLACES)),
            dma((2, 2, PLACES)),
            dma((2, 2, PLACES - 1)),
            dma((PLANE - 1,)),
            dma((PLANE,)),
            dma((max(planes - 1, 1),)),
            dma((planes,)),
            dma((PLANE - 1,)),
            dma((PLANE,)),
        ],
        compiler_params=pltpu.CompilerParams(
            collective_id=0, has_side_effects=True, vmem_limit_bytes=40 * 1024 * 1024
        ),
        cost_estimate=pl.CostEstimate(
            flops=2_500_000_000, bytes_accessed=4_000_000, transcendentals=1_600_000
        ),
    )(*[pltpu.with_memory_space_constraint(x, pltpu.HBM) for x in (queries[0], keys[0], values[0], output_gradient[0], query_down[0].T, value_down[0].T)])
    outs = pl.pallas_call(
        write_out,
        out_shape=tuple(jax.ShapeDtypeStruct(x.shape, x.dtype) for x in outs),
        in_specs=[vmem] * 5,
        out_specs=(hbm,) * 5,
        scratch_shapes=[dma((5,))],
    )(*outs)
    return (outs[0][None], outs[1][None], outs[2][None], outs[3], outs[4])


def solution(mesh):
    spec = P("dp", "ctx", None)
    return jax.shard_map(
        functools.partial(body, mesh.shape["ctx"], mesh.shape["dp"]),
        mesh=mesh,
        in_specs=(spec,) * 6,
        out_specs=(spec, spec, spec, P(), P()),
        check_vma=False,
    )
```

```python
import functools

import jax
import jax.numpy as jnp
from jax import lax
from jax.experimental import pallas as pl
from jax.experimental.pallas import tpu as pltpu
from jax.sharding import PartitionSpec as P

KEY_VALUE_HEADS = 4
PER_HEAD = 8
WIDTH = 128
ROWS = 128
RANK = 16
PLACES = 4
HALF_KEYS = 256
HALF_QUERIES = 2048
PLANE = 8
TILES = 5
KEY_ROWS = slice(0, ROWS)
VALUE_ROWS = slice(ROWS, 2 * ROWS)
DOWN_ROWS = slice(2 * ROWS, 2 * ROWS + RANK)
VALUE_TILE = 2
ADAPTER_SCALE = 2.0
SCALE = WIDTH ** (-0.5)
LOG2E = 1.4426950408889634
MESH = pl.DeviceIdType.MESH
NT = (((1,), (1,)), ((), ()))
NN = (((1,), (0,)), ((), ()))


def matmul(a, b, dims):
    return lax.dot_general(a, b, dims, preferred_element_type=jnp.float32)


def kernel(
    ctx_size, dp_size,
    q_hbm, k_hbm, v_hbm, g_hbm, aq_hbm, av_hbm,
    dq_out, dk_out, dv_out, uq_out, uv_out,
    q_buf, g_buf, aq_buf, kv_buf, w_buf, l_buf,
    part, arrived, l1_send, l1_recv, l2_recv, l3_recv,
    load_sem, own_sem, kv_send, kv_recv, ret_send, ret_recv,
    l1_ssem, l1_rsem, l2_ssem, l2_rsem, l3_ssem, l3_rsem,
):
    i = lax.axis_index("ctx")
    d = lax.axis_index("dp")
    g = i % PLACES
    group = i // PLACES
    parity = g % 2
    first = g // 2
    second = 1 - first
    pairs = dp_size // 2
    me = g * 2 + d % 2
    planes = (ctx_size // PLACES) * pairs
    my_plane = group * pairs + d // 2

    def place_of(h):
        return (g + 2 * h) % PLACES

    def ahead(distance):
        return ((i + distance + ctx_size) % ctx_size, d)

    def plane_peer(e):
        return (group * PLACES + e // 2, (d // 2) * 2 + e % 2)

    def other_plane(r):
        return ((r // pairs) * PLACES + g, (r % pairs) * 2 + d % 2)

    def own_copies(h):
        p = place_of(h)
        cols = pl.ds(pl.multiple_of(h * HALF_KEYS, HALF_KEYS), HALF_KEYS)
        return [
            pltpu.make_async_copy(k_hbm.at[:, cols], kv_buf.at[h, p, KEY_ROWS], own_sem.at[h, 0]),
            pltpu.make_async_copy(v_hbm.at[:, cols], kv_buf.at[h, p, VALUE_ROWS], own_sem.at[h, 1]),
            pltpu.make_async_copy(av_hbm, kv_buf.at[h, p, DOWN_ROWS, pl.ds(0, ROWS)], own_sem.at[h, 2]),
        ]

    def query_copies(h):
        cols = pl.ds(pl.multiple_of(h * HALF_QUERIES, HALF_QUERIES), HALF_QUERIES)
        return [
            pltpu.make_async_copy(q_hbm.at[:, cols], q_buf.at[:, cols], load_sem.at[h, 0]),
            pltpu.make_async_copy(g_hbm.at[:, cols], g_buf.at[:, cols], load_sem.at[h, 1]),
        ]

    rank_copy = pltpu.make_async_copy(aq_hbm, aq_buf, load_sem.at[0, 2])
    for h in (first, second):
        for copy in own_copies(h):
            copy.start()
    for copy in query_copies(first):
        copy.start()
    rank_copy.start()
    for copy in query_copies(second):
        copy.start()

    barrier = pltpu.get_barrier_semaphore()

    def greet(device):
        pl.semaphore_signal(barrier, inc=1, device_id=device, device_id_type=MESH)

    for r in range(1, PLANE):
        greet(plane_peer((me + r) % PLANE))
    for r in range(1, planes):
        greet(other_plane((my_plane + r) % planes))
    beside = (group * PLACES + jnp.where(first == 0, -2, PLACES) + ctx_size) % ctx_size
    greet((beside, d))
    greet((beside + 1, d))
    pl.semaphore_wait(barrier, PLANE - 1 + planes - 1 + 2)

    def key_copy(h, p, distance):
        return pltpu.make_async_remote_copy(
            src_ref=kv_buf.at[h, p],
            dst_ref=kv_buf.at[h, p],
            send_sem=kv_send.at[h, distance - 1],
            recv_sem=kv_recv.at[h, p],
            device_id=ahead(distance),
            device_id_type=MESH,
        )

    def key_arrival(h, b):
        return pltpu.make_async_remote_copy(
            src_ref=kv_buf.at[h, b],
            dst_ref=kv_buf.at[h, b],
            send_sem=kv_send.at[h, 0],
            recv_sem=kv_recv.at[h, b],
            device_id=ahead(1),
            device_id_type=MESH,
        )

    def relay(h):
        return pltpu.make_async_remote_copy(
            src_ref=kv_buf.at[h, 0],
            dst_ref=kv_buf.at[h, 0],
            send_sem=kv_send.at[h, 2],
            recv_sem=kv_recv.at[h, 0],
            device_id=ahead(2),
            device_id_type=MESH,
        )

    for copy in own_copies(first) + own_copies(second):
        copy.wait()
    for distance in range(1, PLACES - 1):
        for h in (first, second):
            p = place_of(h)

            @pl.when(p + distance < PLACES)
            def _():
                key_copy(h, p, distance).start()

    def return_copy(h, c, b, blocks):
        return pltpu.make_async_remote_copy(
            src_ref=part.at[h, c, b],
            dst_ref=arrived.at[h, c, blocks - 2],
            send_sem=ret_send.at[h, c, b],
            recv_sem=ret_recv.at[h, c, blocks - 2],
            device_id=ahead(b - (blocks - 1)),
            device_id_type=MESH,
        )

    def return_arrival(h, c, slot):
        return pltpu.make_async_remote_copy(
            src_ref=arrived.at[h, c, slot],
            dst_ref=arrived.at[h, c, slot],
            send_sem=ret_send.at[h, c, 0],
            recv_sem=ret_recv.at[h, c, slot],
            device_id=ahead(1),
            device_id_type=MESH,
        )

    def l1_copy(r, origin, target):
        return pltpu.make_async_remote_copy(
            src_ref=l1_send.at[target],
            dst_ref=l1_recv.at[origin],
            send_sem=l1_ssem.at[r - 1],
            recv_sem=l1_rsem.at[origin],
            device_id=plane_peer(target),
            device_id_type=MESH,
        )

    def l1_start():
        for r in range(1, PLANE):
            l1_copy(r, me, (me + r) % PLANE).start()

    def head_step(h, c, blocks):
        span = blocks * ROWS
        cols = pl.ds(pl.multiple_of(c * WIDTH, WIDTH), WIDTH)
        base = (2 * h + c) * PER_HEAD * WIDTH

        def head_cols(t):
            return pl.ds(pl.multiple_of(base + t * WIDTH, WIDTH), WIDTH)

        keys = kv_buf[h, :blocks, KEY_ROWS, cols].reshape(span, WIDTH)
        vals = kv_buf[h, :blocks, VALUE_ROWS, cols].reshape(span, WIDTH)
        key_row = lax.broadcasted_iota(jnp.int32, (ROWS, 2 * ROWS), 0)
        query_col = lax.broadcasted_iota(jnp.int32, (ROWS, 2 * ROWS), 1) % ROWS
        allowed = key_row <= query_col

        def pair(buf, t):
            return jnp.concatenate([buf[:, head_cols(2 * t)], buf[:, head_cols(2 * t + 1)]], axis=0)

        for t in range(PER_HEAD // 2):
            q = pair(q_buf, t)
            grad = pair(g_buf, t)
            s = matmul(keys, q, NT)
            last = jnp.where(allowed, s[span - ROWS:], -1e30)
            s = last if blocks == 1 else jnp.concatenate([s[: span - ROWS], last], axis=0)
            top = jnp.max(s, axis=0, keepdims=True)
            score_grad = matmul(vals, grad, NT)
            raised = jnp.exp2((s - top) * (SCALE * LOG2E))
            inverse = 1.0 / jnp.sum(raised, axis=0, keepdims=True)
            delta = jnp.sum(raised * score_grad, axis=0, keepdims=True) * inverse
            probs = raised * inverse
            weights = probs.astype(jnp.bfloat16)
            logit = (probs * (score_grad - delta)).astype(jnp.bfloat16)
            w_buf[:span, 2 * t * ROWS:(2 * t + 2) * ROWS] = weights
            l_buf[:span, 2 * t * ROWS:(2 * t + 2) * ROWS] = logit
        q_all = jnp.concatenate([q_buf[:, head_cols(t)] for t in range(PER_HEAD)], axis=0)
        grad_all = jnp.concatenate([g_buf[:, head_cols(t)] for t in range(PER_HEAD)], axis=0)
        logit_all = l_buf[:span, :]
        dv = matmul(w_buf[:span, :], grad_all, NN).astype(jnp.bfloat16)
        dq = (matmul(keys.T, logit_all, NN) * SCALE).astype(jnp.bfloat16)
        for t in range(PER_HEAD):
            dq_out[:, head_cols(t)] = dq[:, t * ROWS:(t + 1) * ROWS].T
        wide = pl.ds(pl.multiple_of(base, PER_HEAD * WIDTH), PER_HEAD * WIDTH)
        up = matmul(aq_buf[...], dq_out[:, wide], NN).astype(jnp.bfloat16)
        for t in range(PER_HEAD):
            l1_send[t, 3 * h + c] = up[:, t * WIDTH:(t + 1) * WIDTH]
        value_down = jnp.concatenate([kv_buf[h, b, DOWN_ROWS, :ROWS] for b in range(blocks)], axis=1)
        up = matmul(value_down, dv, NN).astype(jnp.bfloat16)
        kv = 2 * h + c
        l1_send[2 * kv, VALUE_TILE] = up
        l1_send[2 * kv + 1, VALUE_TILE] = up
        if blocks > 2:
            pl.when(c == 1)(l1_start)
        dk = (matmul(logit_all, q_all, NN) * SCALE).astype(jnp.bfloat16)
        for b in range(blocks):
            part[h, c, b, 0] = dk[b * ROWS:(b + 1) * ROWS]
            part[h, c, b, 1] = dv[b * ROWS:(b + 1) * ROWS]
        for b in range(blocks - 1):
            return_copy(h, c, b, blocks).start()

    def stage(h, blocks):
        for b in range(blocks - 1):
            key_arrival(h, b).wait_recv()
        if blocks == 2:
            relay(h).start()

        def one(c, carry):
            head_step(h, c, blocks)
            return carry

        lax.fori_loop(0, 2, one, 0)

    for copy in query_copies(first):
        copy.wait()
    rank_copy.wait()
    for blocks in (1, 2):
        pl.when(parity == blocks - 1)(functools.partial(stage, first, blocks))
    for copy in query_copies(second):
        copy.wait()
    for blocks in (3, 4):
        pl.when(parity == blocks - 3)(functools.partial(stage, second, blocks))

    total = l1_send[me].astype(jnp.float32)
    for r in range(1, PLANE):
        e = (me + r) % PLANE
        l1_copy(r, e, me).wait_recv()
        total = total + l1_recv[e].astype(jnp.float32)
    l2_recv[my_plane] = total.astype(jnp.bfloat16)

    def l2_copy(r, origin, target):
        return pltpu.make_async_remote_copy(
            src_ref=l2_recv.at[origin],
            dst_ref=l2_recv.at[origin],
            send_sem=l2_ssem.at[r - 1],
            recv_sem=l2_rsem.at[origin],
            device_id=other_plane(target),
            device_id_type=MESH,
        )

    for r in range(1, planes):
        l2_copy(r, my_plane, (my_plane + r) % planes).start()

    def finish(h, place):
        for c in range(2):
            for slot in range(place, PLACES - 1):
                return_arrival(h, c, slot).wait_recv()
            cols = pl.ds(pl.multiple_of((2 * h + c) * WIDTH, WIDTH), WIDTH)
            for n, out in enumerate((dk_out, dv_out)):
                acc = part[h, c, place, n].astype(jnp.float32)
                for slot in range(place, PLACES - 1):
                    acc = acc + arrived[h, c, slot, n].astype(jnp.float32)
                out[:, cols] = acc.astype(jnp.bfloat16)

    for place in (2, 3):
        pl.when(parity == place - 2)(functools.partial(finish, second, place))

    for r in range(1, planes):
        l2_copy(r, (my_plane + r) % planes, my_plane).wait_recv()
    total = l2_recv[0].astype(jnp.float32)
    for r in range(1, planes):
        total = total + l2_recv[r].astype(jnp.float32)
    l3_recv[me] = (total * ADAPTER_SCALE).astype(jnp.bfloat16)

    def l3_copy(r, origin, target):
        return pltpu.make_async_remote_copy(
            src_ref=l3_recv.at[origin],
            dst_ref=l3_recv.at[origin],
            send_sem=l3_ssem.at[r - 1],
            recv_sem=l3_rsem.at[origin],
            device_id=plane_peer(target),
            device_id_type=MESH,
        )

    for r in range(1, PLANE):
        l3_copy(r, me, (me + r) % PLANE).start()
    for place in (0, 1):
        pl.when(parity == place)(functools.partial(finish, first, place))
    for r in range(1, PLANE):
        l3_copy(r, (me + r) % PLANE, me).wait_recv()
    for e in range(PLANE):
        for kv in range(KEY_VALUE_HEADS):
            head = kv * PER_HEAD + e
            uq_out[:, head * WIDTH:(head + 1) * WIDTH] = l3_recv[e, kv + kv // 2].astype(jnp.float32)
    for kv in range(KEY_VALUE_HEADS):
        uv_out[:, kv * WIDTH:(kv + 1) * WIDTH] = l3_recv[2 * kv, VALUE_TILE].astype(jnp.float32)

    pl.when(parity == 1)(lambda: relay(first).wait_send())
    for h in (first, second):
        p = place_of(h)
        for distance in range(1, PLACES - 1):

            @pl.when(p + distance < PLACES)
            def _():
                key_copy(h, p, distance).wait_send()

    def returned(h, blocks):
        for c in range(2):
            for b in range(blocks - 1):
                return_copy(h, c, b, blocks).wait_send()

    pl.when(parity == 1)(functools.partial(returned, first, 2))
    for blocks in (3, 4):
        pl.when(parity == blocks - 3)(functools.partial(returned, second, blocks))
    for r in range(1, PLANE):
        l1_copy(r, me, (me + r) % PLANE).wait_send()
        l3_copy(r, me, (me + r) % PLANE).wait_send()
    for r in range(1, planes):
        l2_copy(r, my_plane, (my_plane + r) % planes).wait_send()


def write_out(*refs):
    sources, targets, sems = refs[:5], refs[5:10], refs[10]
    copies = [
        pltpu.make_async_copy(source, target, sems.at[n])
        for n, (source, target) in enumerate(zip(sources, targets))
    ]
    for copy in copies:
        copy.start()
    for copy in copies:
        copy.wait()


def body(ctx_size, dp_size, queries, keys, values, output_gradient, query_down, value_down):
    planes = (ctx_size // PLACES) * (dp_size // 2)
    bf16, f32 = jnp.bfloat16, jnp.float32
    dma = pltpu.SemaphoreType.DMA
    hbm = pl.BlockSpec(memory_space=pltpu.HBM)
    vmem = pl.BlockSpec(memory_space=pltpu.VMEM)
    wide = PER_HEAD * WIDTH
    outs = pl.pallas_call(
        functools.partial(kernel, ctx_size, dp_size),
        out_shape=(
            pltpu.VMEM(queries.shape[1:], bf16),
            pltpu.VMEM(keys.shape[1:], bf16),
            pltpu.VMEM(values.shape[1:], bf16),
            pltpu.VMEM((RANK, queries.shape[2]), f32),
            pltpu.VMEM((RANK, values.shape[2]), f32),
        ),
        in_specs=[hbm] * 6,
        out_specs=(vmem,) * 5,
        scratch_shapes=[
            pltpu.VMEM((ROWS, KEY_VALUE_HEADS * wide), bf16),
            pltpu.VMEM((ROWS, KEY_VALUE_HEADS * wide), bf16),
            pltpu.VMEM((RANK, ROWS), bf16),
            pltpu.VMEM((2, PLACES, 2 * ROWS + RANK, HALF_KEYS), bf16),
            pltpu.VMEM((PLACES * ROWS, wide), bf16),
            pltpu.VMEM((PLACES * ROWS, wide), bf16),
            pltpu.VMEM((2, 2, PLACES, 2, ROWS, WIDTH), bf16),
            pltpu.VMEM((2, 2, PLACES - 1, 2, ROWS, WIDTH), bf16),
            pltpu.VMEM((PLANE, TILES, RANK, WIDTH), bf16),
            pltpu.VMEM((PLANE, TILES, RANK, WIDTH), bf16),
            pltpu.VMEM((planes, TILES, RANK, WIDTH), bf16),
            pltpu.VMEM((PLANE, TILES, RANK, WIDTH), bf16),
            dma((2, 3)),
            dma((2, 3)),
            dma((2, PLACES - 1)),
            dma((2, PLACES)),
            dma((2, 2, PLACES)),
            dma((2, 2, PLACES - 1)),
            dma((PLANE - 1,)),
            dma((PLANE,)),
            dma((max(planes - 1, 1),)),
            dma((planes,)),
            dma((PLANE - 1,)),
            dma((PLANE,)),
        ],
        compiler_params=pltpu.CompilerParams(
            collective_id=0, has_side_effects=True, vmem_limit_bytes=40 * 1024 * 1024
        ),
        cost_estimate=pl.CostEstimate(
            flops=2_500_000_000, bytes_accessed=4_000_000, transcendentals=1_600_000
        ),
    )(*[pltpu.with_memory_space_constraint(x, pltpu.HBM) for x in (queries[0], keys[0], values[0], output_gradient[0], query_down[0].T, value_down[0].T)])
    outs = pl.pallas_call(
        write_out,
        out_shape=tuple(jax.ShapeDtypeStruct(x.shape, x.dtype) for x in outs),
        in_specs=[vmem] * 5,
        out_specs=(hbm,) * 5,
        scratch_shapes=[dma((5,))],
    )(*[pltpu.with_memory_space_constraint(x, pltpu.VMEM) for x in outs])
    return (outs[0][None], outs[1][None], outs[2][None], outs[3], outs[4])


def solution(mesh):
    spec = P("dp", "ctx", None)
    return jax.shard_map(
        functools.partial(body, mesh.shape["ctx"], mesh.shape["dp"]),
        mesh=mesh,
        in_specs=(spec,) * 6,
        out_specs=(spec, spec, spec, P(), P()),
        check_vma=False,
    )
```

```python
import functools

import jax
import jax.numpy as jnp
from jax import lax
from jax.experimental import pallas as pl
from jax.experimental.pallas import tpu as pltpu
from jax.sharding import PartitionSpec as P

KEY_VALUE_HEADS = 4
PER_HEAD = 8
WIDTH = 128
ROWS = 128
RANK = 16
PLACES = 4
HALF_KEYS = 256
HALF_QUERIES = 2048
PLANE = 8
TILES = 5
KEY_ROWS = slice(0, ROWS)
VALUE_ROWS = slice(ROWS, 2 * ROWS)
DOWN_ROWS = slice(2 * ROWS, 2 * ROWS + RANK)
VALUE_TILE = 2
ADAPTER_SCALE = 2.0
SCALE = WIDTH ** (-0.5)
LOG2E = 1.4426950408889634
MESH = pl.DeviceIdType.MESH
NT = (((1,), (1,)), ((), ()))
NN = (((1,), (0,)), ((), ()))


def matmul(a, b, dims):
    return lax.dot_general(a, b, dims, preferred_element_type=jnp.float32)


def kernel(
    ctx_size, dp_size,
    q_hbm, k_hbm, v_hbm, g_hbm, aq_hbm, av_hbm,
    dq_out, dk_out, dv_out, uq_out, uv_out,
    q_buf, g_buf, aq_buf, kv_buf, w_buf, l_buf,
    part, arrived, l1_send, l1_recv, l2_recv, l3_recv,
    load_sem, own_sem, kv_send, kv_recv, ret_send, ret_recv,
    l1_ssem, l1_rsem, l2_ssem, l2_rsem, l3_ssem, l3_rsem,
):
    i = lax.axis_index("ctx")
    d = lax.axis_index("dp")
    g = i % PLACES
    group = i // PLACES
    parity = g % 2
    first = g // 2
    second = 1 - first
    pairs = dp_size // 2
    me = g * 2 + d % 2
    planes = (ctx_size // PLACES) * pairs
    my_plane = group * pairs + d // 2

    def place_of(h):
        return (g + 2 * h) % PLACES

    def ahead(distance):
        return ((i + distance + ctx_size) % ctx_size, d)

    def plane_peer(e):
        return (group * PLACES + e // 2, (d // 2) * 2 + e % 2)

    def other_plane(r):
        return ((r // pairs) * PLACES + g, (r % pairs) * 2 + d % 2)

    def own_copies(h):
        p = place_of(h)
        cols = pl.ds(pl.multiple_of(h * HALF_KEYS, HALF_KEYS), HALF_KEYS)
        return [
            pltpu.make_async_copy(k_hbm.at[:, cols], kv_buf.at[h, p, KEY_ROWS], own_sem.at[h, 0]),
            pltpu.make_async_copy(v_hbm.at[:, cols], kv_buf.at[h, p, VALUE_ROWS], own_sem.at[h, 1]),
            pltpu.make_async_copy(av_hbm, kv_buf.at[h, p, DOWN_ROWS, pl.ds(0, ROWS)], own_sem.at[h, 2]),
        ]

    def query_copies(h):
        cols = pl.ds(pl.multiple_of(h * HALF_QUERIES, HALF_QUERIES), HALF_QUERIES)
        return [
            pltpu.make_async_copy(q_hbm.at[:, cols], q_buf.at[:, cols], load_sem.at[h, 0]),
            pltpu.make_async_copy(g_hbm.at[:, cols], g_buf.at[:, cols], load_sem.at[h, 1]),
        ]

    rank_copy = pltpu.make_async_copy(aq_hbm, aq_buf, load_sem.at[0, 2])
    for h in (first, second):
        for copy in own_copies(h):
            copy.start()
    for copy in query_copies(first):
        copy.start()
    rank_copy.start()
    for copy in query_copies(second):
        copy.start()

    barrier = pltpu.get_barrier_semaphore()

    def greet(device):
        pl.semaphore_signal(barrier, inc=1, device_id=device, device_id_type=MESH)

    for r in range(1, PLANE):
        greet(plane_peer((me + r) % PLANE))
    for r in range(1, planes):
        greet(other_plane((my_plane + r) % planes))
    beside = (group * PLACES + jnp.where(first == 0, -2, PLACES) + ctx_size) % ctx_size
    greet((beside, d))
    greet((beside + 1, d))
    pl.semaphore_wait(barrier, PLANE - 1 + planes - 1 + 2)

    def key_copy(h, p, distance):
        return pltpu.make_async_remote_copy(
            src_ref=kv_buf.at[h, p],
            dst_ref=kv_buf.at[h, p],
            send_sem=kv_send.at[h, distance - 1],
            recv_sem=kv_recv.at[h, p],
            device_id=ahead(distance),
            device_id_type=MESH,
        )

    def key_arrival(h, b):
        return pltpu.make_async_remote_copy(
            src_ref=kv_buf.at[h, b],
            dst_ref=kv_buf.at[h, b],
            send_sem=kv_send.at[h, 0],
            recv_sem=kv_recv.at[h, b],
            device_id=ahead(1),
            device_id_type=MESH,
        )

    def relay(h):
        return pltpu.make_async_remote_copy(
            src_ref=kv_buf.at[h, 0],
            dst_ref=kv_buf.at[h, 0],
            send_sem=kv_send.at[h, 2],
            recv_sem=kv_recv.at[h, 0],
            device_id=ahead(2),
            device_id_type=MESH,
        )

    for copy in own_copies(first) + own_copies(second):
        copy.wait()
    for distance in range(1, PLACES - 1):
        for h in (first, second):
            p = place_of(h)

            @pl.when(p + distance < PLACES)
            def _():
                key_copy(h, p, distance).start()

    def return_copy(h, c, b, blocks):
        return pltpu.make_async_remote_copy(
            src_ref=part.at[h, c, b],
            dst_ref=arrived.at[h, c, blocks - 2],
            send_sem=ret_send.at[h, c, b],
            recv_sem=ret_recv.at[h, c, blocks - 2],
            device_id=ahead(b - (blocks - 1)),
            device_id_type=MESH,
        )

    def return_arrival(h, c, slot):
        return pltpu.make_async_remote_copy(
            src_ref=arrived.at[h, c, slot],
            dst_ref=arrived.at[h, c, slot],
            send_sem=ret_send.at[h, c, 0],
            recv_sem=ret_recv.at[h, c, slot],
            device_id=ahead(1),
            device_id_type=MESH,
        )

    def l1_copy(r, origin, target):
        return pltpu.make_async_remote_copy(
            src_ref=l1_send.at[target],
            dst_ref=l1_recv.at[origin],
            send_sem=l1_ssem.at[r - 1],
            recv_sem=l1_rsem.at[origin],
            device_id=plane_peer(target),
            device_id_type=MESH,
        )

    def l1_start():
        for r in range(1, PLANE):
            l1_copy(r, me, (me + r) % PLANE).start()

    def head_step(h, c, blocks):
        span = blocks * ROWS
        cols = pl.ds(pl.multiple_of(c * WIDTH, WIDTH), WIDTH)
        base = (2 * h + c) * PER_HEAD * WIDTH

        def head_cols(t):
            return pl.ds(pl.multiple_of(base + t * WIDTH, WIDTH), WIDTH)

        keys = kv_buf[h, :blocks, KEY_ROWS, cols].reshape(span, WIDTH)
        vals = kv_buf[h, :blocks, VALUE_ROWS, cols].reshape(span, WIDTH)
        key_row = lax.broadcasted_iota(jnp.int32, (ROWS, 2 * ROWS), 0)
        query_col = lax.broadcasted_iota(jnp.int32, (ROWS, 2 * ROWS), 1) % ROWS
        allowed = key_row <= query_col

        def pair(buf, t):
            return jnp.concatenate([buf[:, head_cols(2 * t)], buf[:, head_cols(2 * t + 1)]], axis=0)

        def pair_step(t, carry):
            q = pair(q_buf, t)
            grad = pair(g_buf, t)
            s = matmul(keys, q, NT)
            last = jnp.where(allowed, s[span - ROWS:], -1e30)
            s = last if blocks == 1 else jnp.concatenate([s[: span - ROWS], last], axis=0)
            top = jnp.max(s, axis=0, keepdims=True)
            score_grad = matmul(vals, grad, NT)
            raised = jnp.exp2((s - top) * (SCALE * LOG2E))
            inverse = 1.0 / jnp.sum(raised, axis=0, keepdims=True)
            delta = jnp.sum(raised * score_grad, axis=0, keepdims=True) * inverse
            probs = raised * inverse
            weights = probs.astype(jnp.bfloat16)
            logit = (probs * (score_grad - delta)).astype(jnp.bfloat16)
            place = pl.ds(pl.multiple_of(2 * t * ROWS, 2 * ROWS), 2 * ROWS)
            w_buf[:span, place] = weights
            l_buf[:span, place] = logit
            return carry

        lax.fori_loop(0, PER_HEAD // 2, pair_step, 0)
        q_all = jnp.concatenate([q_buf[:, head_cols(t)] for t in range(PER_HEAD)], axis=0)
        grad_all = jnp.concatenate([g_buf[:, head_cols(t)] for t in range(PER_HEAD)], axis=0)
        logit_all = l_buf[:span, :]
        dv = matmul(w_buf[:span, :], grad_all, NN).astype(jnp.bfloat16)
        dq = (matmul(keys.T, logit_all, NN) * SCALE).astype(jnp.bfloat16)
        for t in range(PER_HEAD):
            dq_out[:, head_cols(t)] = dq[:, t * ROWS:(t + 1) * ROWS].T
        wide = pl.ds(pl.multiple_of(base, PER_HEAD * WIDTH), PER_HEAD * WIDTH)
        up = matmul(aq_buf[...], dq_out[:, wide], NN).astype(jnp.bfloat16)
        for t in range(PER_HEAD):
            l1_send[t, 3 * h + c] = up[:, t * WIDTH:(t + 1) * WIDTH]
        value_down = jnp.concatenate([kv_buf[h, b, DOWN_ROWS, :ROWS] for b in range(blocks)], axis=1)
        up = matmul(value_down, dv, NN).astype(jnp.bfloat16)
        kv = 2 * h + c
        l1_send[2 * kv, VALUE_TILE] = up
        l1_send[2 * kv + 1, VALUE_TILE] = up
        if blocks > 2:
            pl.when(c == 1)(l1_start)
        dk = (matmul(logit_all, q_all, NN) * SCALE).astype(jnp.bfloat16)
        for b in range(blocks):
            part[h, c, b, 0] = dk[b * ROWS:(b + 1) * ROWS]
            part[h, c, b, 1] = dv[b * ROWS:(b + 1) * ROWS]
        for b in range(blocks - 1):
            return_copy(h, c, b, blocks).start()

    def stage(h, blocks):
        for b in range(blocks - 1):
            key_arrival(h, b).wait_recv()
        if blocks == 2:
            relay(h).start()

        def one(c, carry):
            head_step(h, c, blocks)
            return carry

        lax.fori_loop(0, 2, one, 0)

    for copy in query_copies(first):
        copy.wait()
    rank_copy.wait()
    for blocks in (1, 2):
        pl.when(parity == blocks - 1)(functools.partial(stage, first, blocks))
    for copy in query_copies(second):
        copy.wait()
    for blocks in (3, 4):
        pl.when(parity == blocks - 3)(functools.partial(stage, second, blocks))

    total = l1_send[me].astype(jnp.float32)
    for r in range(1, PLANE):
        e = (me + r) % PLANE
        l1_copy(r, e, me).wait_recv()
        total = total + l1_recv[e].astype(jnp.float32)
    l2_recv[my_plane] = total.astype(jnp.bfloat16)

    def l2_copy(r, origin, target):
        return pltpu.make_async_remote_copy(
            src_ref=l2_recv.at[origin],
            dst_ref=l2_recv.at[origin],
            send_sem=l2_ssem.at[r - 1],
            recv_sem=l2_rsem.at[origin],
            device_id=other_plane(target),
            device_id_type=MESH,
        )

    for r in range(1, planes):
        l2_copy(r, my_plane, (my_plane + r) % planes).start()

    def finish(h, place):
        for c in range(2):
            for slot in range(place, PLACES - 1):
                return_arrival(h, c, slot).wait_recv()
            cols = pl.ds(pl.multiple_of((2 * h + c) * WIDTH, WIDTH), WIDTH)
            for n, out in enumerate((dk_out, dv_out)):
                acc = part[h, c, place, n].astype(jnp.float32)
                for slot in range(place, PLACES - 1):
                    acc = acc + arrived[h, c, slot, n].astype(jnp.float32)
                out[:, cols] = acc.astype(jnp.bfloat16)

    for place in (2, 3):
        pl.when(parity == place - 2)(functools.partial(finish, second, place))

    for r in range(1, planes):
        l2_copy(r, (my_plane + r) % planes, my_plane).wait_recv()
    total = l2_recv[0].astype(jnp.float32)
    for r in range(1, planes):
        total = total + l2_recv[r].astype(jnp.float32)
    l3_recv[me] = (total * ADAPTER_SCALE).astype(jnp.bfloat16)

    def l3_copy(r, origin, target):
        return pltpu.make_async_remote_copy(
            src_ref=l3_recv.at[origin],
            dst_ref=l3_recv.at[origin],
            send_sem=l3_ssem.at[r - 1],
            recv_sem=l3_rsem.at[origin],
            device_id=plane_peer(target),
            device_id_type=MESH,
        )

    for r in range(1, PLANE):
        l3_copy(r, me, (me + r) % PLANE).start()
    for place in (0, 1):
        pl.when(parity == place)(functools.partial(finish, first, place))
    for r in range(1, PLANE):
        l3_copy(r, (me + r) % PLANE, me).wait_recv()
    for e in range(PLANE):
        for kv in range(KEY_VALUE_HEADS):
            head = kv * PER_HEAD + e
            uq_out[:, head * WIDTH:(head + 1) * WIDTH] = l3_recv[e, kv + kv // 2].astype(jnp.float32)
    for kv in range(KEY_VALUE_HEADS):
        uv_out[:, kv * WIDTH:(kv + 1) * WIDTH] = l3_recv[2 * kv, VALUE_TILE].astype(jnp.float32)

    pl.when(parity == 1)(lambda: relay(first).wait_send())
    for h in (first, second):
        p = place_of(h)
        for distance in range(1, PLACES - 1):

            @pl.when(p + distance < PLACES)
            def _():
                key_copy(h, p, distance).wait_send()

    def returned(h, blocks):
        for c in range(2):
            for b in range(blocks - 1):
                return_copy(h, c, b, blocks).wait_send()

    pl.when(parity == 1)(functools.partial(returned, first, 2))
    for blocks in (3, 4):
        pl.when(parity == blocks - 3)(functools.partial(returned, second, blocks))
    for r in range(1, PLANE):
        l1_copy(r, me, (me + r) % PLANE).wait_send()
        l3_copy(r, me, (me + r) % PLANE).wait_send()
    for r in range(1, planes):
        l2_copy(r, my_plane, (my_plane + r) % planes).wait_send()


def write_out(*refs):
    sources, targets, sems = refs[:5], refs[5:10], refs[10]
    copies = [
        pltpu.make_async_copy(source, target, sems.at[n])
        for n, (source, target) in enumerate(zip(sources, targets))
    ]
    for copy in copies:
        copy.start()
    for copy in copies:
        copy.wait()


def body(ctx_size, dp_size, queries, keys, values, output_gradient, query_down, value_down):
    planes = (ctx_size // PLACES) * (dp_size // 2)
    bf16, f32 = jnp.bfloat16, jnp.float32
    dma = pltpu.SemaphoreType.DMA
    hbm = pl.BlockSpec(memory_space=pltpu.HBM)
    vmem = pl.BlockSpec(memory_space=pltpu.VMEM)
    wide = PER_HEAD * WIDTH
    outs = pl.pallas_call(
        functools.partial(kernel, ctx_size, dp_size),
        out_shape=(
            pltpu.VMEM(queries.shape[1:], bf16),
            pltpu.VMEM(keys.shape[1:], bf16),
            pltpu.VMEM(values.shape[1:], bf16),
            pltpu.VMEM((RANK, queries.shape[2]), f32),
            pltpu.VMEM((RANK, values.shape[2]), f32),
        ),
        in_specs=[hbm] * 6,
        out_specs=(vmem,) * 5,
        scratch_shapes=[
            pltpu.VMEM((ROWS, KEY_VALUE_HEADS * wide), bf16),
            pltpu.VMEM((ROWS, KEY_VALUE_HEADS * wide), bf16),
            pltpu.VMEM((RANK, ROWS), bf16),
            pltpu.VMEM((2, PLACES, 2 * ROWS + RANK, HALF_KEYS), bf16),
            pltpu.VMEM((PLACES * ROWS, wide), bf16),
            pltpu.VMEM((PLACES * ROWS, wide), bf16),
            pltpu.VMEM((2, 2, PLACES, 2, ROWS, WIDTH), bf16),
            pltpu.VMEM((2, 2, PLACES - 1, 2, ROWS, WIDTH), bf16),
            pltpu.VMEM((PLANE, TILES, RANK, WIDTH), bf16),
            pltpu.VMEM((PLANE, TILES, RANK, WIDTH), bf16),
            pltpu.VMEM((planes, TILES, RANK, WIDTH), bf16),
            pltpu.VMEM((PLANE, TILES, RANK, WIDTH), bf16),
            dma((2, 3)),
            dma((2, 3)),
            dma((2, PLACES - 1)),
            dma((2, PLACES)),
            dma((2, 2, PLACES)),
            dma((2, 2, PLACES - 1)),
            dma((PLANE - 1,)),
            dma((PLANE,)),
            dma((max(planes - 1, 1),)),
            dma((planes,)),
            dma((PLANE - 1,)),
            dma((PLANE,)),
        ],
        compiler_params=pltpu.CompilerParams(
            collective_id=0, has_side_effects=True, vmem_limit_bytes=40 * 1024 * 1024
        ),
        cost_estimate=pl.CostEstimate(
            flops=2_500_000_000, bytes_accessed=4_000_000, transcendentals=1_600_000
        ),
    )(*[pltpu.with_memory_space_constraint(x, pltpu.HBM) for x in (queries[0], keys[0], values[0], output_gradient[0], query_down[0].T, value_down[0].T)])
    outs = pl.pallas_call(
        write_out,
        out_shape=tuple(jax.ShapeDtypeStruct(x.shape, x.dtype) for x in outs),
        in_specs=[vmem] * 5,
        out_specs=(hbm,) * 5,
        scratch_shapes=[dma((5,))],
    )(*[pltpu.with_memory_space_constraint(x, pltpu.VMEM) for x in outs])
    return (outs[0][None], outs[1][None], outs[2][None], outs[3], outs[4])


def solution(mesh):
    spec = P("dp", "ctx", None)
    return jax.shard_map(
        functools.partial(body, mesh.shape["ctx"], mesh.shape["dp"]),
        mesh=mesh,
        in_specs=(spec,) * 6,
        out_specs=(spec, spec, spec, P(), P()),
        check_vma=False,
    )
```

```python
import functools

import jax
import jax.numpy as jnp
from jax import lax
from jax.experimental import pallas as pl
from jax.experimental.pallas import tpu as pltpu
from jax.sharding import PartitionSpec as P

KEY_VALUE_HEADS = 4
PER_HEAD = 8
WIDTH = 128
ROWS = 128
RANK = 16
PLACES = 4
HALF_KEYS = 256
HALF_QUERIES = 2048
PLANE = 8
TILES = 5
KEY_ROWS = slice(0, ROWS)
VALUE_ROWS = slice(ROWS, 2 * ROWS)
DOWN_ROWS = slice(2 * ROWS, 2 * ROWS + RANK)
VALUE_TILE = 2
ADAPTER_SCALE = 2.0
SCALE = WIDTH ** (-0.5)
LOG2E = 1.4426950408889634
MESH = pl.DeviceIdType.MESH
NT = (((1,), (1,)), ((), ()))
NN = (((1,), (0,)), ((), ()))


def matmul(a, b, dims):
    return lax.dot_general(a, b, dims, preferred_element_type=jnp.float32)


def kernel(
    ctx_size, dp_size,
    q_hbm, k_hbm, v_hbm, g_hbm, aq_hbm, av_hbm,
    dq_out, dk_out, dv_out, uq_out, uv_out,
    q_buf, g_buf, aq_buf, kv_buf, w_buf, l_buf,
    part, arrived, l1_send, l1_recv, l2_recv, l3_recv,
    load_sem, own_sem, kv_send, kv_recv, ret_send, ret_recv,
    l1_ssem, l1_rsem, l2_ssem, l2_rsem, l3_ssem, l3_rsem,
):
    i = lax.axis_index("ctx")
    d = lax.axis_index("dp")
    g = i % PLACES
    group = i // PLACES
    parity = g % 2
    first = g // 2
    second = 1 - first
    pairs = dp_size // 2
    me = g * 2 + d % 2
    planes = (ctx_size // PLACES) * pairs
    my_plane = group * pairs + d // 2

    def place_of(h):
        return (g + 2 * h) % PLACES

    def ahead(distance):
        return ((i + distance + ctx_size) % ctx_size, d)

    def plane_peer(e):
        return (group * PLACES + e // 2, (d // 2) * 2 + e % 2)

    def other_plane(r):
        return ((r // pairs) * PLACES + g, (r % pairs) * 2 + d % 2)

    def own_copies(h):
        p = place_of(h)
        cols = pl.ds(pl.multiple_of(h * HALF_KEYS, HALF_KEYS), HALF_KEYS)
        return [
            pltpu.make_async_copy(k_hbm.at[:, cols], kv_buf.at[h, p, KEY_ROWS], own_sem.at[h, 0]),
            pltpu.make_async_copy(v_hbm.at[:, cols], kv_buf.at[h, p, VALUE_ROWS], own_sem.at[h, 1]),
            pltpu.make_async_copy(av_hbm, kv_buf.at[h, p, DOWN_ROWS, pl.ds(0, ROWS)], own_sem.at[h, 2]),
        ]

    def query_copies(h):
        cols = pl.ds(pl.multiple_of(h * HALF_QUERIES, HALF_QUERIES), HALF_QUERIES)
        return [
            pltpu.make_async_copy(q_hbm.at[:, cols], q_buf.at[:, cols], load_sem.at[h, 0]),
            pltpu.make_async_copy(g_hbm.at[:, cols], g_buf.at[:, cols], load_sem.at[h, 1]),
        ]

    rank_copy = pltpu.make_async_copy(aq_hbm, aq_buf, load_sem.at[0, 2])
    for h in (first, second):
        for copy in own_copies(h):
            copy.start()
    for copy in query_copies(first):
        copy.start()
    rank_copy.start()
    for copy in query_copies(second):
        copy.start()

    barrier = pltpu.get_barrier_semaphore()

    def greet(device):
        pl.semaphore_signal(barrier, inc=1, device_id=device, device_id_type=MESH)

    for r in range(1, PLANE):
        greet(plane_peer((me + r) % PLANE))
    for r in range(1, planes):
        greet(other_plane((my_plane + r) % planes))
    beside = (group * PLACES + jnp.where(first == 0, -2, PLACES) + ctx_size) % ctx_size
    greet((beside, d))
    greet((beside + 1, d))
    pl.semaphore_wait(barrier, PLANE - 1 + planes - 1 + 2)

    def key_copy(h, p, distance):
        return pltpu.make_async_remote_copy(
            src_ref=kv_buf.at[h, p],
            dst_ref=kv_buf.at[h, p],
            send_sem=kv_send.at[h, distance - 1],
            recv_sem=kv_recv.at[h, p],
            device_id=ahead(distance),
            device_id_type=MESH,
        )

    def key_arrival(h, b):
        return pltpu.make_async_remote_copy(
            src_ref=kv_buf.at[h, b],
            dst_ref=kv_buf.at[h, b],
            send_sem=kv_send.at[h, 0],
            recv_sem=kv_recv.at[h, b],
            device_id=ahead(1),
            device_id_type=MESH,
        )

    def relay(h):
        return pltpu.make_async_remote_copy(
            src_ref=kv_buf.at[h, 0],
            dst_ref=kv_buf.at[h, 0],
            send_sem=kv_send.at[h, 2],
            recv_sem=kv_recv.at[h, 0],
            device_id=ahead(2),
            device_id_type=MESH,
        )

    for copy in own_copies(first) + own_copies(second):
        copy.wait()
    for distance in range(1, PLACES - 1):
        for h in (first, second):
            p = place_of(h)

            @pl.when(p + distance < PLACES)
            def _():
                key_copy(h, p, distance).start()

    def return_copy(h, c, b, blocks):
        return pltpu.make_async_remote_copy(
            src_ref=part.at[h, c, b],
            dst_ref=arrived.at[h, c, blocks - 2],
            send_sem=ret_send.at[h, c, b],
            recv_sem=ret_recv.at[h, c, blocks - 2],
            device_id=ahead(b - (blocks - 1)),
            device_id_type=MESH,
        )

    def return_arrival(h, c, slot):
        return pltpu.make_async_remote_copy(
            src_ref=arrived.at[h, c, slot],
            dst_ref=arrived.at[h, c, slot],
            send_sem=ret_send.at[h, c, 0],
            recv_sem=ret_recv.at[h, c, slot],
            device_id=ahead(1),
            device_id_type=MESH,
        )

    def l1_copy(n, origin, half, r, target):
        tiles = pl.ds(3 * half, 2) if n == 0 else pl.ds(2 * half, 3)
        return pltpu.make_async_remote_copy(
            src_ref=l1_send.at[target, tiles],
            dst_ref=l1_recv.at[origin, tiles],
            send_sem=l1_ssem.at[n, r - 1],
            recv_sem=l1_rsem.at[n, origin],
            device_id=plane_peer(target),
            device_id_type=MESH,
        )

    def l1_start(n, half):
        for r in range(1, PLANE):
            l1_copy(n, me, half, r, (me + r) % PLANE).start()

    def head_step(h, c, blocks):
        span = blocks * ROWS
        cols = pl.ds(pl.multiple_of(c * WIDTH, WIDTH), WIDTH)
        base = (2 * h + c) * PER_HEAD * WIDTH

        def head_cols(t):
            return pl.ds(pl.multiple_of(base + t * WIDTH, WIDTH), WIDTH)

        keys = kv_buf[h, :blocks, KEY_ROWS, cols].reshape(span, WIDTH)
        vals = kv_buf[h, :blocks, VALUE_ROWS, cols].reshape(span, WIDTH)
        key_row = lax.broadcasted_iota(jnp.int32, (ROWS, 2 * ROWS), 0)
        query_col = lax.broadcasted_iota(jnp.int32, (ROWS, 2 * ROWS), 1) % ROWS
        allowed = key_row <= query_col

        def pair(buf, t):
            return jnp.concatenate([buf[:, head_cols(2 * t)], buf[:, head_cols(2 * t + 1)]], axis=0)

        for t in range(PER_HEAD // 2):
            q = pair(q_buf, t)
            grad = pair(g_buf, t)
            s = matmul(keys, q, NT)
            last = jnp.where(allowed, s[span - ROWS:], -1e30)
            s = last if blocks == 1 else jnp.concatenate([s[: span - ROWS], last], axis=0)
            top = jnp.max(s, axis=0, keepdims=True)
            score_grad = matmul(vals, grad, NT)
            raised = jnp.exp2((s - top) * (SCALE * LOG2E))
            inverse = 1.0 / jnp.sum(raised, axis=0, keepdims=True)
            delta = jnp.sum(raised * score_grad, axis=0, keepdims=True) * inverse
            probs = raised * inverse
            weights = probs.astype(jnp.bfloat16)
            logit = (probs * (score_grad - delta)).astype(jnp.bfloat16)
            w_buf[:span, 2 * t * ROWS:(2 * t + 2) * ROWS] = weights
            l_buf[:span, 2 * t * ROWS:(2 * t + 2) * ROWS] = logit
        q_all = jnp.concatenate([q_buf[:, head_cols(t)] for t in range(PER_HEAD)], axis=0)
        grad_all = jnp.concatenate([g_buf[:, head_cols(t)] for t in range(PER_HEAD)], axis=0)
        logit_all = l_buf[:span, :]
        dv = matmul(w_buf[:span, :], grad_all, NN).astype(jnp.bfloat16)
        dq = (matmul(keys.T, logit_all, NN) * SCALE).astype(jnp.bfloat16)
        for t in range(PER_HEAD):
            dq_out[:, head_cols(t)] = dq[:, t * ROWS:(t + 1) * ROWS].T
        wide = pl.ds(pl.multiple_of(base, PER_HEAD * WIDTH), PER_HEAD * WIDTH)
        up = matmul(aq_buf[...], dq_out[:, wide], NN).astype(jnp.bfloat16)
        for t in range(PER_HEAD):
            l1_send[t, 3 * h + c] = up[:, t * WIDTH:(t + 1) * WIDTH]
        value_down = jnp.concatenate([kv_buf[h, b, DOWN_ROWS, :ROWS] for b in range(blocks)], axis=1)
        up = matmul(value_down, dv, NN).astype(jnp.bfloat16)
        kv = 2 * h + c
        l1_send[2 * kv, VALUE_TILE] = up
        l1_send[2 * kv + 1, VALUE_TILE] = up
        if blocks > 2:
            pl.when(c == 1)(functools.partial(l1_start, 1, h))
        dk = (matmul(logit_all, q_all, NN) * SCALE).astype(jnp.bfloat16)
        for b in range(blocks):
            part[h, c, b, 0] = dk[b * ROWS:(b + 1) * ROWS]
            part[h, c, b, 1] = dv[b * ROWS:(b + 1) * ROWS]
        if blocks == 2:
            return_copy(h, c, 0, blocks).start()
        elif blocks > 2:

            @pl.when(c == 0)
            def _():
                for b in range(blocks - 1):
                    return_copy(h, c, b, blocks).start()

    def stage(h, blocks):
        for b in range(blocks - 1):
            key_arrival(h, b).wait_recv()
        if blocks == 2:
            relay(h).start()

        def one(c, carry):
            head_step(h, c, blocks)
            return carry

        lax.fori_loop(0, 2, one, 0)

    for copy in query_copies(first):
        copy.wait()
    rank_copy.wait()
    for blocks in (1, 2):
        pl.when(parity == blocks - 1)(functools.partial(stage, first, blocks))
    l1_start(0, first)
    for copy in query_copies(second):
        copy.wait()
    for blocks in (3, 4):
        pl.when(parity == blocks - 3)(functools.partial(stage, second, blocks))

    total = l1_send[me].astype(jnp.float32)
    for r in range(1, PLANE):
        e = (me + r) % PLANE
        l1_copy(0, e, e // 4, r, me).wait_recv()
        l1_copy(1, e, 1 - e // 4, r, me).wait_recv()
        total = total + l1_recv[e].astype(jnp.float32)
    l2_recv[my_plane] = total.astype(jnp.bfloat16)

    def l2_copy(r, origin, target):
        return pltpu.make_async_remote_copy(
            src_ref=l2_recv.at[origin],
            dst_ref=l2_recv.at[origin],
            send_sem=l2_ssem.at[r - 1],
            recv_sem=l2_rsem.at[origin],
            device_id=other_plane(target),
            device_id_type=MESH,
        )

    for r in range(1, planes):
        l2_copy(r, my_plane, (my_plane + r) % planes).start()

    def last_returns(blocks):
        for b in range(blocks - 1):
            return_copy(second, 1, b, blocks).start()

    for blocks in (3, 4):
        pl.when(parity == blocks - 3)(functools.partial(last_returns, blocks))

    def finish(h, place):
        for c in range(2):
            for slot in range(place, PLACES - 1):
                return_arrival(h, c, slot).wait_recv()
            cols = pl.ds(pl.multiple_of((2 * h + c) * WIDTH, WIDTH), WIDTH)
            for n, out in enumerate((dk_out, dv_out)):
                acc = part[h, c, place, n].astype(jnp.float32)
                for slot in range(place, PLACES - 1):
                    acc = acc + arrived[h, c, slot, n].astype(jnp.float32)
                out[:, cols] = acc.astype(jnp.bfloat16)

    for r in range(1, planes):
        l2_copy(r, (my_plane + r) % planes, my_plane).wait_recv()
    total = l2_recv[0].astype(jnp.float32)
    for r in range(1, planes):
        total = total + l2_recv[r].astype(jnp.float32)
    l3_recv[me] = (total * ADAPTER_SCALE).astype(jnp.bfloat16)

    def l3_copy(r, origin, target):
        return pltpu.make_async_remote_copy(
            src_ref=l3_recv.at[origin],
            dst_ref=l3_recv.at[origin],
            send_sem=l3_ssem.at[r - 1],
            recv_sem=l3_rsem.at[origin],
            device_id=plane_peer(target),
            device_id_type=MESH,
        )

    for r in range(1, PLANE):
        l3_copy(r, me, (me + r) % PLANE).start()
    for place in (2, 3):
        pl.when(parity == place - 2)(functools.partial(finish, second, place))
    for place in (0, 1):
        pl.when(parity == place)(functools.partial(finish, first, place))
    for r in range(1, PLANE):
        l3_copy(r, (me + r) % PLANE, me).wait_recv()
    for e in range(PLANE):
        for kv in range(KEY_VALUE_HEADS):
            head = kv * PER_HEAD + e
            uq_out[:, head * WIDTH:(head + 1) * WIDTH] = l3_recv[e, kv + kv // 2].astype(jnp.float32)
    for kv in range(KEY_VALUE_HEADS):
        uv_out[:, kv * WIDTH:(kv + 1) * WIDTH] = l3_recv[2 * kv, VALUE_TILE].astype(jnp.float32)

    pl.when(parity == 1)(lambda: relay(first).wait_send())
    for h in (first, second):
        p = place_of(h)
        for distance in range(1, PLACES - 1):

            @pl.when(p + distance < PLACES)
            def _():
                key_copy(h, p, distance).wait_send()

    def returned(h, blocks):
        for c in range(2):
            for b in range(blocks - 1):
                return_copy(h, c, b, blocks).wait_send()

    pl.when(parity == 1)(functools.partial(returned, first, 2))
    for blocks in (3, 4):
        pl.when(parity == blocks - 3)(functools.partial(returned, second, blocks))
    for r in range(1, PLANE):
        l1_copy(0, me, first, r, (me + r) % PLANE).wait_send()
        l1_copy(1, me, second, r, (me + r) % PLANE).wait_send()
        l3_copy(r, me, (me + r) % PLANE).wait_send()
    for r in range(1, planes):
        l2_copy(r, my_plane, (my_plane + r) % planes).wait_send()


def write_out(*refs):
    sources, targets, sems = refs[:5], refs[5:10], refs[10]
    copies = [
        pltpu.make_async_copy(source, target, sems.at[n])
        for n, (source, target) in enumerate(zip(sources, targets))
    ]
    for copy in copies:
        copy.start()
    for copy in copies:
        copy.wait()


def body(ctx_size, dp_size, queries, keys, values, output_gradient, query_down, value_down):
    planes = (ctx_size // PLACES) * (dp_size // 2)
    bf16, f32 = jnp.bfloat16, jnp.float32
    dma = pltpu.SemaphoreType.DMA
    hbm = pl.BlockSpec(memory_space=pltpu.HBM)
    vmem = pl.BlockSpec(memory_space=pltpu.VMEM)
    wide = PER_HEAD * WIDTH
    outs = pl.pallas_call(
        functools.partial(kernel, ctx_size, dp_size),
        out_shape=(
            pltpu.VMEM(queries.shape[1:], bf16),
            pltpu.VMEM(keys.shape[1:], bf16),
            pltpu.VMEM(values.shape[1:], bf16),
            pltpu.VMEM((RANK, queries.shape[2]), f32),
            pltpu.VMEM((RANK, values.shape[2]), f32),
        ),
        in_specs=[hbm] * 6,
        out_specs=(vmem,) * 5,
        scratch_shapes=[
            pltpu.VMEM((ROWS, KEY_VALUE_HEADS * wide), bf16),
            pltpu.VMEM((ROWS, KEY_VALUE_HEADS * wide), bf16),
            pltpu.VMEM((RANK, ROWS), bf16),
            pltpu.VMEM((2, PLACES, 2 * ROWS + RANK, HALF_KEYS), bf16),
            pltpu.VMEM((PLACES * ROWS, wide), bf16),
            pltpu.VMEM((PLACES * ROWS, wide), bf16),
            pltpu.VMEM((2, 2, PLACES, 2, ROWS, WIDTH), bf16),
            pltpu.VMEM((2, 2, PLACES - 1, 2, ROWS, WIDTH), bf16),
            pltpu.VMEM((PLANE, TILES, RANK, WIDTH), bf16),
            pltpu.VMEM((PLANE, TILES, RANK, WIDTH), bf16),
            pltpu.VMEM((planes, TILES, RANK, WIDTH), bf16),
            pltpu.VMEM((PLANE, TILES, RANK, WIDTH), bf16),
            dma((2, 3)),
            dma((2, 3)),
            dma((2, PLACES - 1)),
            dma((2, PLACES)),
            dma((2, 2, PLACES)),
            dma((2, 2, PLACES - 1)),
            dma((2, PLANE - 1)),
            dma((2, PLANE)),
            dma((max(planes - 1, 1),)),
            dma((planes,)),
            dma((PLANE - 1,)),
            dma((PLANE,)),
        ],
        compiler_params=pltpu.CompilerParams(
            collective_id=0, has_side_effects=True, vmem_limit_bytes=40 * 1024 * 1024
        ),
        cost_estimate=pl.CostEstimate(
            flops=2_500_000_000, bytes_accessed=4_000_000, transcendentals=1_600_000
        ),
    )(*[pltpu.with_memory_space_constraint(x, pltpu.HBM) for x in (queries[0], keys[0], values[0], output_gradient[0], query_down[0].T, value_down[0].T)])
    outs = pl.pallas_call(
        write_out,
        out_shape=tuple(jax.ShapeDtypeStruct(x.shape, x.dtype) for x in outs),
        in_specs=[vmem] * 5,
        out_specs=(hbm,) * 5,
        scratch_shapes=[dma((5,))],
    )(*[pltpu.with_memory_space_constraint(x, pltpu.VMEM) for x in outs])
    return (outs[0][None], outs[1][None], outs[2][None], outs[3], outs[4])


def solution(mesh):
    spec = P("dp", "ctx", None)
    return jax.shard_map(
        functools.partial(body, mesh.shape["ctx"], mesh.shape["dp"]),
        mesh=mesh,
        in_specs=(spec,) * 6,
        out_specs=(spec, spec, spec, P(), P()),
        check_vma=False,
    )
```

```python
import functools

import jax
import jax.numpy as jnp
from jax import lax
from jax.experimental import pallas as pl
from jax.experimental.pallas import tpu as pltpu
from jax.sharding import PartitionSpec as P

KEY_VALUE_HEADS = 4
PER_HEAD = 8
WIDTH = 128
ROWS = 128
RANK = 16
PLACES = 4
HALF_QUERIES = 2048
PLANE = 8
TILES = 5
KEY_ROWS = slice(0, ROWS)
VALUE_ROWS = slice(ROWS, 2 * ROWS)
DOWN_ROWS = slice(2 * ROWS, 2 * ROWS + RANK)
VALUE_TILE = 2
ADAPTER_SCALE = 2.0
SCALE = WIDTH ** (-0.5)
LOG2E = 1.4426950408889634
MESH = pl.DeviceIdType.MESH
NT = (((1,), (1,)), ((), ()))
NN = (((1,), (0,)), ((), ()))


def matmul(a, b, dims):
    return lax.dot_general(a, b, dims, preferred_element_type=jnp.float32)


def kernel(
    ctx_size, dp_size,
    q_hbm, k_hbm, v_hbm, g_hbm, aq_hbm, av_hbm,
    dq_out, dk_out, dv_out, uq_out, uv_out,
    q_buf, g_buf, aq_buf, kv_buf, w_buf, l_buf,
    part, arrived, l1_send, l1_recv, l2_recv, l3_recv,
    load_sem, own_sem, kv_send, kv_recv, ret_send, ret_recv,
    l1_ssem, l1_rsem, l2_ssem, l2_rsem, l3_ssem, l3_rsem,
):
    i = lax.axis_index("ctx")
    d = lax.axis_index("dp")
    g = i % PLACES
    group = i // PLACES
    parity = g % 2
    first = g // 2
    second = 1 - first
    pairs = dp_size // 2
    me = g * 2 + d % 2
    planes = (ctx_size // PLACES) * pairs
    my_plane = group * pairs + d // 2

    def place_of(h):
        return (g + 2 * h) % PLACES

    def ahead(distance):
        return ((i + distance + ctx_size) % ctx_size, d)

    def plane_peer(e):
        return (group * PLACES + e // 2, (d // 2) * 2 + e % 2)

    def other_plane(r):
        return ((r // pairs) * PLACES + g, (r % pairs) * 2 + d % 2)

    def own_copies(h, c):
        p = place_of(h)
        cols = pl.ds(pl.multiple_of((2 * h + c) * WIDTH, WIDTH), WIDTH)
        return [
            pltpu.make_async_copy(k_hbm.at[:, cols], kv_buf.at[h, c, p, KEY_ROWS], own_sem.at[h, c, 0]),
            pltpu.make_async_copy(v_hbm.at[:, cols], kv_buf.at[h, c, p, VALUE_ROWS], own_sem.at[h, c, 1]),
            pltpu.make_async_copy(av_hbm, kv_buf.at[h, c, p, DOWN_ROWS], own_sem.at[h, c, 2]),
        ]

    def query_copies(h):
        cols = pl.ds(pl.multiple_of(h * HALF_QUERIES, HALF_QUERIES), HALF_QUERIES)
        return [
            pltpu.make_async_copy(q_hbm.at[:, cols], q_buf.at[:, cols], load_sem.at[h, 0]),
            pltpu.make_async_copy(g_hbm.at[:, cols], g_buf.at[:, cols], load_sem.at[h, 1]),
        ]

    rank_copy = pltpu.make_async_copy(aq_hbm, aq_buf, load_sem.at[0, 2])
    for c in range(2):
        for h in (first, second):
            for copy in own_copies(h, c):
                copy.start()
    for copy in query_copies(first):
        copy.start()
    rank_copy.start()
    for copy in query_copies(second):
        copy.start()

    barrier = pltpu.get_barrier_semaphore()

    def greet(device):
        pl.semaphore_signal(barrier, inc=1, device_id=device, device_id_type=MESH)

    for r in range(1, PLANE):
        greet(plane_peer((me + r) % PLANE))
    for r in range(1, planes):
        greet(other_plane((my_plane + r) % planes))
    beside = (group * PLACES + jnp.where(first == 0, -2, PLACES) + ctx_size) % ctx_size
    greet((beside, d))
    greet((beside + 1, d))
    pl.semaphore_wait(barrier, PLANE - 1 + planes - 1 + 2)

    def key_copy(h, c, p, distance):
        return pltpu.make_async_remote_copy(
            src_ref=kv_buf.at[h, c, p],
            dst_ref=kv_buf.at[h, c, p],
            send_sem=kv_send.at[h, c, distance - 1],
            recv_sem=kv_recv.at[h, c, p],
            device_id=ahead(distance),
            device_id_type=MESH,
        )

    def key_arrival(h, c, b):
        return pltpu.make_async_remote_copy(
            src_ref=kv_buf.at[h, c, b],
            dst_ref=kv_buf.at[h, c, b],
            send_sem=kv_send.at[h, c, 0],
            recv_sem=kv_recv.at[h, c, b],
            device_id=ahead(1),
            device_id_type=MESH,
        )

    def relay(h, c):
        return pltpu.make_async_remote_copy(
            src_ref=kv_buf.at[h, c, 0],
            dst_ref=kv_buf.at[h, c, 0],
            send_sem=kv_send.at[h, c, 2],
            recv_sem=kv_recv.at[h, c, 0],
            device_id=ahead(2),
            device_id_type=MESH,
        )

    for c in range(2):
        for copy in own_copies(first, c) + own_copies(second, c):
            copy.wait()
        for distance in range(1, PLACES - 1):
            for h in (first, second):
                p = place_of(h)

                @pl.when(p + distance < PLACES)
                def _():
                    key_copy(h, c, p, distance).start()

    def return_copy(h, c, b, blocks):
        return pltpu.make_async_remote_copy(
            src_ref=part.at[h, c, b],
            dst_ref=arrived.at[h, c, blocks - 2],
            send_sem=ret_send.at[h, c, b],
            recv_sem=ret_recv.at[h, c, blocks - 2],
            device_id=ahead(b - (blocks - 1)),
            device_id_type=MESH,
        )

    def return_arrival(h, c, slot):
        return pltpu.make_async_remote_copy(
            src_ref=arrived.at[h, c, slot],
            dst_ref=arrived.at[h, c, slot],
            send_sem=ret_send.at[h, c, 0],
            recv_sem=ret_recv.at[h, c, slot],
            device_id=ahead(1),
            device_id_type=MESH,
        )

    def l1_copy(r, origin, target):
        return pltpu.make_async_remote_copy(
            src_ref=l1_send.at[target],
            dst_ref=l1_recv.at[origin],
            send_sem=l1_ssem.at[r - 1],
            recv_sem=l1_rsem.at[origin],
            device_id=plane_peer(target),
            device_id_type=MESH,
        )

    def l1_start():
        for r in range(1, PLANE):
            l1_copy(r, me, (me + r) % PLANE).start()

    def head_step(h, c, blocks):
        span = blocks * ROWS
        base = (2 * h + c) * PER_HEAD * WIDTH

        def head_cols(t):
            return pl.ds(pl.multiple_of(base + t * WIDTH, WIDTH), WIDTH)

        keys = kv_buf[h, c, :blocks, KEY_ROWS, :].reshape(span, WIDTH)
        vals = kv_buf[h, c, :blocks, VALUE_ROWS, :].reshape(span, WIDTH)
        key_row = lax.broadcasted_iota(jnp.int32, (ROWS, 2 * ROWS), 0)
        query_col = lax.broadcasted_iota(jnp.int32, (ROWS, 2 * ROWS), 1) % ROWS
        allowed = key_row <= query_col

        def pair(buf, t):
            return jnp.concatenate([buf[:, head_cols(2 * t)], buf[:, head_cols(2 * t + 1)]], axis=0)

        for t in range(PER_HEAD // 2):
            q = pair(q_buf, t)
            grad = pair(g_buf, t)
            s = matmul(keys, q, NT)
            last = jnp.where(allowed, s[span - ROWS:], -1e30)
            s = last if blocks == 1 else jnp.concatenate([s[: span - ROWS], last], axis=0)
            top = jnp.max(s, axis=0, keepdims=True)
            score_grad = matmul(vals, grad, NT)
            raised = jnp.exp2((s - top) * (SCALE * LOG2E))
            inverse = 1.0 / jnp.sum(raised, axis=0, keepdims=True)
            delta = jnp.sum(raised * score_grad, axis=0, keepdims=True) * inverse
            probs = raised * inverse
            weights = probs.astype(jnp.bfloat16)
            logit = (probs * (score_grad - delta)).astype(jnp.bfloat16)
            w_buf[:span, 2 * t * ROWS:(2 * t + 2) * ROWS] = weights
            l_buf[:span, 2 * t * ROWS:(2 * t + 2) * ROWS] = logit
        q_all = jnp.concatenate([q_buf[:, head_cols(t)] for t in range(PER_HEAD)], axis=0)
        grad_all = jnp.concatenate([g_buf[:, head_cols(t)] for t in range(PER_HEAD)], axis=0)
        logit_all = l_buf[:span, :]
        dv = matmul(w_buf[:span, :], grad_all, NN).astype(jnp.bfloat16)
        dq = (matmul(keys.T, logit_all, NN) * SCALE).astype(jnp.bfloat16)
        for t in range(PER_HEAD):
            dq_out[:, head_cols(t)] = dq[:, t * ROWS:(t + 1) * ROWS].T
        wide = pl.ds(pl.multiple_of(base, PER_HEAD * WIDTH), PER_HEAD * WIDTH)
        up = matmul(aq_buf[...], dq_out[:, wide], NN).astype(jnp.bfloat16)
        for t in range(PER_HEAD):
            l1_send[t, 3 * h + c] = up[:, t * WIDTH:(t + 1) * WIDTH]
        value_down = jnp.concatenate([kv_buf[h, c, b, DOWN_ROWS, :] for b in range(blocks)], axis=1)
        up = matmul(value_down, dv, NN).astype(jnp.bfloat16)
        kv = 2 * h + c
        l1_send[2 * kv, VALUE_TILE] = up
        l1_send[2 * kv + 1, VALUE_TILE] = up
        if blocks > 2:
            pl.when(c == 1)(l1_start)
        dk = (matmul(logit_all, q_all, NN) * SCALE).astype(jnp.bfloat16)
        for b in range(blocks):
            part[h, c, b, 0] = dk[b * ROWS:(b + 1) * ROWS]
            part[h, c, b, 1] = dv[b * ROWS:(b + 1) * ROWS]
        for b in range(blocks - 1):
            return_copy(h, c, b, blocks).start()

    def stage(h, blocks):
        def one(c, carry):
            for b in range(blocks - 1):
                key_arrival(h, c, b).wait_recv()
            if blocks == 2:
                relay(h, c).start()
            head_step(h, c, blocks)
            return carry

        lax.fori_loop(0, 2, one, 0)

    for copy in query_copies(first):
        copy.wait()
    rank_copy.wait()
    for blocks in (1, 2):
        pl.when(parity == blocks - 1)(functools.partial(stage, first, blocks))
    for copy in query_copies(second):
        copy.wait()
    for blocks in (3, 4):
        pl.when(parity == blocks - 3)(functools.partial(stage, second, blocks))

    total = l1_send[me].astype(jnp.float32)
    for r in range(1, PLANE):
        e = (me + r) % PLANE
        l1_copy(r, e, me).wait_recv()
        total = total + l1_recv[e].astype(jnp.float32)
    l2_recv[my_plane] = total.astype(jnp.bfloat16)

    def l2_copy(r, origin, target):
        return pltpu.make_async_remote_copy(
            src_ref=l2_recv.at[origin],
            dst_ref=l2_recv.at[origin],
            send_sem=l2_ssem.at[r - 1],
            recv_sem=l2_rsem.at[origin],
            device_id=other_plane(target),
            device_id_type=MESH,
        )

    for r in range(1, planes):
        l2_copy(r, my_plane, (my_plane + r) % planes).start()

    def finish(h, place):
        for c in range(2):
            for slot in range(place, PLACES - 1):
                return_arrival(h, c, slot).wait_recv()
            cols = pl.ds(pl.multiple_of((2 * h + c) * WIDTH, WIDTH), WIDTH)
            for n, out in enumerate((dk_out, dv_out)):
                acc = part[h, c, place, n].astype(jnp.float32)
                for slot in range(place, PLACES - 1):
                    acc = acc + arrived[h, c, slot, n].astype(jnp.float32)
                out[:, cols] = acc.astype(jnp.bfloat16)

    for place in (2, 3):
        pl.when(parity == place - 2)(functools.partial(finish, second, place))

    for r in range(1, planes):
        l2_copy(r, (my_plane + r) % planes, my_plane).wait_recv()
    total = l2_recv[0].astype(jnp.float32)
    for r in range(1, planes):
        total = total + l2_recv[r].astype(jnp.float32)
    l3_recv[me] = (total * ADAPTER_SCALE).astype(jnp.bfloat16)

    def l3_copy(r, origin, target):
        return pltpu.make_async_remote_copy(
            src_ref=l3_recv.at[origin],
            dst_ref=l3_recv.at[origin],
            send_sem=l3_ssem.at[r - 1],
            recv_sem=l3_rsem.at[origin],
            device_id=plane_peer(target),
            device_id_type=MESH,
        )

    for r in range(1, PLANE):
        l3_copy(r, me, (me + r) % PLANE).start()
    for place in (0, 1):
        pl.when(parity == place)(functools.partial(finish, first, place))
    for r in range(1, PLANE):
        l3_copy(r, (me + r) % PLANE, me).wait_recv()
    for e in range(PLANE):
        for kv in range(KEY_VALUE_HEADS):
            head = kv * PER_HEAD + e
            uq_out[:, head * WIDTH:(head + 1) * WIDTH] = l3_recv[e, kv + kv // 2].astype(jnp.float32)
    for kv in range(KEY_VALUE_HEADS):
        uv_out[:, kv * WIDTH:(kv + 1) * WIDTH] = l3_recv[2 * kv, VALUE_TILE].astype(jnp.float32)

    @pl.when(parity == 1)
    def _():
        for c in range(2):
            relay(first, c).wait_send()

    for h in (first, second):
        p = place_of(h)
        for distance in range(1, PLACES - 1):

            @pl.when(p + distance < PLACES)
            def _():
                for c in range(2):
                    key_copy(h, c, p, distance).wait_send()

    def returned(h, blocks):
        for c in range(2):
            for b in range(blocks - 1):
                return_copy(h, c, b, blocks).wait_send()

    pl.when(parity == 1)(functools.partial(returned, first, 2))
    for blocks in (3, 4):
        pl.when(parity == blocks - 3)(functools.partial(returned, second, blocks))
    for r in range(1, PLANE):
        l1_copy(r, me, (me + r) % PLANE).wait_send()
        l3_copy(r, me, (me + r) % PLANE).wait_send()
    for r in range(1, planes):
        l2_copy(r, my_plane, (my_plane + r) % planes).wait_send()


def write_out(*refs):
    sources, targets, sems = refs[:5], refs[5:10], refs[10]
    copies = [
        pltpu.make_async_copy(source, target, sems.at[n])
        for n, (source, target) in enumerate(zip(sources, targets))
    ]
    for copy in copies:
        copy.start()
    for copy in copies:
        copy.wait()


def body(ctx_size, dp_size, queries, keys, values, output_gradient, query_down, value_down):
    planes = (ctx_size // PLACES) * (dp_size // 2)
    bf16, f32 = jnp.bfloat16, jnp.float32
    dma = pltpu.SemaphoreType.DMA
    hbm = pl.BlockSpec(memory_space=pltpu.HBM)
    vmem = pl.BlockSpec(memory_space=pltpu.VMEM)
    wide = PER_HEAD * WIDTH
    outs = pl.pallas_call(
        functools.partial(kernel, ctx_size, dp_size),
        out_shape=(
            pltpu.VMEM(queries.shape[1:], bf16),
            pltpu.VMEM(keys.shape[1:], bf16),
            pltpu.VMEM(values.shape[1:], bf16),
            pltpu.VMEM((RANK, queries.shape[2]), f32),
            pltpu.VMEM((RANK, values.shape[2]), f32),
        ),
        in_specs=[hbm] * 6,
        out_specs=(vmem,) * 5,
        scratch_shapes=[
            pltpu.VMEM((ROWS, KEY_VALUE_HEADS * wide), bf16),
            pltpu.VMEM((ROWS, KEY_VALUE_HEADS * wide), bf16),
            pltpu.VMEM((RANK, ROWS), bf16),
            pltpu.VMEM((2, 2, PLACES, 2 * ROWS + RANK, WIDTH), bf16),
            pltpu.VMEM((PLACES * ROWS, wide), bf16),
            pltpu.VMEM((PLACES * ROWS, wide), bf16),
            pltpu.VMEM((2, 2, PLACES, 2, ROWS, WIDTH), bf16),
            pltpu.VMEM((2, 2, PLACES - 1, 2, ROWS, WIDTH), bf16),
            pltpu.VMEM((PLANE, TILES, RANK, WIDTH), bf16),
            pltpu.VMEM((PLANE, TILES, RANK, WIDTH), bf16),
            pltpu.VMEM((planes, TILES, RANK, WIDTH), bf16),
            pltpu.VMEM((PLANE, TILES, RANK, WIDTH), bf16),
            dma((2, 3)),
            dma((2, 2, 3)),
            dma((2, 2, PLACES - 1)),
            dma((2, 2, PLACES)),
            dma((2, 2, PLACES)),
            dma((2, 2, PLACES - 1)),
            dma((PLANE - 1,)),
            dma((PLANE,)),
            dma((max(planes - 1, 1),)),
            dma((planes,)),
            dma((PLANE - 1,)),
            dma((PLANE,)),
        ],
        compiler_params=pltpu.CompilerParams(
            collective_id=0, has_side_effects=True, vmem_limit_bytes=40 * 1024 * 1024
        ),
        cost_estimate=pl.CostEstimate(
            flops=2_500_000_000, bytes_accessed=4_000_000, transcendentals=1_600_000
        ),
    )(*[pltpu.with_memory_space_constraint(x, pltpu.HBM) for x in (queries[0], keys[0], values[0], output_gradient[0], query_down[0].T, value_down[0].T)])
    outs = pl.pallas_call(
        write_out,
        out_shape=tuple(jax.ShapeDtypeStruct(x.shape, x.dtype) for x in outs),
        in_specs=[vmem] * 5,
        out_specs=(hbm,) * 5,
        scratch_shapes=[dma((5,))],
    )(*[pltpu.with_memory_space_constraint(x, pltpu.VMEM) for x in outs])
    return (outs[0][None], outs[1][None], outs[2][None], outs[3], outs[4])


def solution(mesh):
    spec = P("dp", "ctx", None)
    return jax.shard_map(
        functools.partial(body, mesh.shape["ctx"], mesh.shape["dp"]),
        mesh=mesh,
        in_specs=(spec,) * 6,
        out_specs=(spec, spec, spec, P(), P()),
        check_vma=False,
    )
```
